256 devices in a mesh: dp: 4 (over y_lo, core), context: 32 (over x, z), tensor: 2 (over y_hi).
Axes of the slice: x: 4, y: 4 (y_hi: 2, y_lo: 2; y = y_hi * 2 + y_lo), z: 8, core: 2. Of those that a mesh axis runs over, the one named last changes fastest.
Arguments:
- queries: bfloat16 [16384, 2560], P(('dp', 'context'), 'tensor'), may hold values from -6 to 6
- key_rows: bfloat16 [16384, 2560], P(('dp', 'context'), 'tensor'), may hold values from -6 to 6
- value_rows: bfloat16 [16384, 2560], P(('dp', 'context'), 'tensor'), may hold values from -6 to 6
- gate_rows: bfloat16 [16384, 2560], P(('dp', 'context'), 'tensor'), may hold values from -6 to 6
- out_grad: bfloat16 [16384, 2560], P(('dp', 'context'), 'tensor'), may hold values from -6 to 6
- decay_rate: float32 [10], P('tensor'), may hold values from 3.0517578e-05 to 0.03125
- norm_gain: float32 [2560], P('tensor'), may hold values from 0.5 to 1.5
- reset_offsets: int32 [4, 16], P('dp'), may hold values from 0 to 128, as said below
- pair_prompts: int32 [4, 2], P('dp'), may hold values from 0 to 15
Outputs:
- retained: bfloat16 [16384, 2560], P(('dp', 'context'), 'tensor')
- grad_query: bfloat16 [16384, 2560], P(('dp', 'context'), 'tensor')
- grad_key: bfloat16 [16384, 2560], P(('dp', 'context'), 'tensor')
- grad_value: bfloat16 [16384, 2560], P(('dp', 'context'), 'tensor')
- grad_gate: bfloat16 [16384, 2560], P(('dp', 'context'), 'tensor')
- grad_gain: float32 [2560], P('tensor')
The draws below stay inside these ranges and needn't reach their ends.
Inputs may be any that keep to these rules, and one draw needn't show every extreme that they name: `reset_offsets`: 128 means that no document starts in the shard.
All inputs are finite; a program needn't handle non-finite values.
Results may differ from the reference program's by a relative error of at most 0.0053.
Values sent between devices are 32-bit elements; how exact they have to be, the bound alone decides.
A program may use at most 128 MiB of HBM per device.

```python
import math
import jax
import jax.numpy as jnp
from jax import lax

HEADS = 10
HEAD_DIM = 256
TOK_DEV = 128
CH = 2560
PROMPT_SHARDS = 16
SPAN = 4
PAIRS = 2
TOKENS = 16384
N_DP = 4
N_CONTEXT = 32


def draw_reset_offsets(key, part):
    key = jax.random.fold_in(key, 11)
    key_mask, key_spot, key_low, key_high = jax.random.split(key, 4)
    entry_count = N_DP * PROMPT_SHARDS
    resets_here = jax.random.randint(key_mask, (entry_count,), 0, 3) == 0
    offsets = jax.random.randint(key_spot, (entry_count,), 0, TOK_DEV)
    values = jnp.where(resets_here, offsets, TOK_DEV)
    lowest_at = jax.random.randint(key_low, (), 0, entry_count)
    highest_at = (lowest_at + 1 + jax.random.randint(key_high, (), 0, entry_count - 1)) % entry_count
    values = values.at[lowest_at].set(0).at[highest_at].set(TOK_DEV)
    return values.reshape(N_DP, PROMPT_SHARDS).astype(jnp.int32)


def draw_pair_prompts(key, part):
    key = jax.random.fold_in(key, 23)
    key_pick, key_low, key_high = jax.random.split(key, 3)
    entry_count = N_DP * PAIRS
    values = jax.random.randint(key_pick, (entry_count,), 0, PROMPT_SHARDS)
    lowest_at = jax.random.randint(key_low, (), 0, entry_count)
    highest_at = (lowest_at + 1 + jax.random.randint(key_high, (), 0, entry_count - 1)) % entry_count
    values = values.at[lowest_at].set(0).at[highest_at].set(PROMPT_SHARDS - 1)
    return values.reshape(N_DP, PAIRS).astype(jnp.int32)


def steps_of(own_key, extent, shards, least, largest):
    gain = 1.0
    for dim, parts in shards:
        heights = jax.random.uniform(jax.random.fold_in(jax.random.fold_in(own_key, 6), dim), (parts,), jnp.float32, least / len(shards), largest / len(shards))
        gain = gain * jnp.repeat(jnp.exp(heights), extent[dim] // parts).reshape((-1,) + (1,) * (len(extent) - 1 - dim))
    return gain


def scatter_about(own_key, shape, scale, bound, pieces=(), held_as=jnp.bfloat16):
    factor_of = steps_of(own_key, shape, pieces, -0.22, 0.18) if pieces else 1.0
    drawn = jax.random.normal(own_key, shape, jnp.float32) * scale * factor_of
    return jnp.minimum(jnp.maximum(drawn, -bound), bound).astype(held_as)


def setup_inputs(seed: int = 0) -> dict:
    arg_keys = jax.random.split(jax.random.key(seed), 10)
    queries = scatter_about(arg_keys[0], (TOKENS, CH), 1.0, 6.0, ((0, 128), (1, 2)))
    key_rows = scatter_about(arg_keys[1], (TOKENS, CH), 1.0, 6.0, ((0, 128), (1, 2)))
    value_rows = scatter_about(arg_keys[2], (TOKENS, CH), 1.0, 6.0, ((0, 128), (1, 2)))
    gate_rows = scatter_about(arg_keys[3], (TOKENS, CH), 1.0, 6.0, ((0, 128), (1, 2)))
    out_grad = scatter_about(arg_keys[4], (TOKENS, CH), 1.0, 6.0, ((0, 128), (1, 2)))
    decay_rate = jnp.clip(jnp.exp(math.log(0.03125) - 6.931472 * jax.random.uniform(arg_keys[5], (HEADS,), jnp.float32) ** steps_of(arg_keys[5], (HEADS,), ((0, 2),), -0.2, 0.2)), 3.0517578125e-05, 0.03125)
    norm_gain = jnp.clip(1.0 + 0.1 * jax.random.normal(arg_keys[6], (CH,), jnp.float32), 0.5, 1.5)
    reset_offsets = draw_reset_offsets(jax.random.fold_in(arg_keys[9], 71), 0)
    pair_prompts = draw_pair_prompts(jax.random.fold_in(arg_keys[9], 71), 0)
    return dict(queries=queries, key_rows=key_rows, value_rows=value_rows, gate_rows=gate_rows, out_grad=out_grad, decay_rate=decay_rate, norm_gain=norm_gain, reset_offsets=reset_offsets, pair_prompts=pair_prompts)


def decay_tables(decay_rate, reset_point, length):
    positions = jnp.arange(length, dtype=jnp.int32)
    position_float = positions.astype(jnp.float32)
    later_doc = positions >= reset_point
    distance = position_float[:, None] - position_float[None, :]
    allowed = (distance >= 0.0) & (later_doc[:, None] == later_doc[None, :])
    decay_mask = jnp.where(allowed[None], jnp.exp(-decay_rate[:, None, None] * jnp.maximum(distance, 0.0)[None]), 0.0)
    into_weight = jnp.where((positions < reset_point)[None], jnp.exp(-decay_rate[:, None] * (position_float + 1.0)[None]), 0.0)
    out_weight = jnp.where((positions >= reset_point % length)[None], jnp.exp(-decay_rate[:, None] * (length - 1.0 - position_float)[None]), 0.0)
    link_decay = jnp.where(reset_point == length, jnp.exp(-decay_rate * length), 0.0)
    return (decay_mask, into_weight.T[:, :, None], out_weight.T[:, :, None], link_decay)

def finish(mixed, gate_value, gain_grid):
    centre = mixed - lax.optimization_barrier(jnp.mean(mixed, axis=-1, keepdims=True))
    spread = lax.optimization_barrier(jnp.mean(centre * centre, axis=-1, keepdims=True))
    return jax.nn.silu(gate_value) * (centre * lax.rsqrt(spread + 1e-05)) * gain_grid

def reference(queries, key_rows, value_rows, gate_rows, out_grad, decay_rate, norm_gain, reset_offsets, pair_prompts):
    grid_shape = (N_DP, N_CONTEXT, TOK_DEV, HEADS, HEAD_DIM)
    key_scale = HEAD_DIM ** (-0.5)
    gain_grid = norm_gain.reshape(HEADS, HEAD_DIM)
    quarter = N_CONTEXT // 4
    shard_index = jnp.arange(N_CONTEXT, dtype=jnp.int32)
    is_prompt = (shard_index >= quarter) & (shard_index < quarter + PROMPT_SHARDS)
    response_index = jnp.where(is_prompt, 0, jnp.where(shard_index < quarter, shard_index, shard_index - PROMPT_SHARDS))
    shard_depth = jnp.where(is_prompt, 0, response_index % SPAN)
    first_flags = jnp.logical_or(jnp.logical_and(jnp.logical_not(is_prompt), shard_depth == 0), shard_index == quarter)
    pair_index = jnp.where(is_prompt, -1, response_index // (2 * SPAN))
    seed_lift = jnp.where(is_prompt[:, None], 0.0, jnp.exp(-decay_rate[None, :] * (TOK_DEV * shard_depth).astype(jnp.float32)[:, None]))
    pair_slots = jnp.arange(PAIRS, dtype=jnp.int32)
    state_shape = (HEADS, HEAD_DIM, HEAD_DIM)

    def shard_state(shard_item):
        key_part, value_part, reset_point = shard_item
        decay_mask, into_weight, out_weight, link_decay = decay_tables(decay_rate, reset_point, TOK_DEV)
        scaled_keys = key_part.astype(jnp.float32) * out_weight
        local_state = key_scale * jnp.einsum('shd,she->hde', scaled_keys, value_part.astype(jnp.float32), precision=lax.Precision.HIGHEST)
        return (local_state, link_decay)

    def shard_forward(shard_item):
        query_part, key_part, value_part, gate_part, grad_part, reset_point, state_in = shard_item
        decay_mask, into_weight, out_weight, link_decay = decay_tables(decay_rate, reset_point, TOK_DEV)
        query_float = query_part.astype(jnp.float32)
        scores = jnp.einsum('thd,shd->hts', query_float, key_part.astype(jnp.float32)) * key_scale
        weights = (scores * decay_mask).astype(jnp.bfloat16)
        lifted = query_float * into_weight
        mixed = jnp.einsum('hts,shd->thd', weights.astype(jnp.float32), value_part.astype(jnp.float32))
        mixed = mixed + jnp.einsum('thd,hde->the', lifted, state_in, precision=lax.Precision.HIGHEST)
        retained_full, pullback = jax.vjp(finish, mixed, gate_part.astype(jnp.float32), gain_grid)
        grad_mixed, grad_gate, gain_part = pullback(grad_part.astype(jnp.float32))
        entry_grad = jnp.einsum('thd,the->hde', lifted, grad_mixed, precision=lax.Precision.HIGHEST)
        return (retained_full.astype(jnp.bfloat16), grad_mixed, grad_gate.astype(jnp.bfloat16), gain_part, entry_grad)

    def shard_backward(shard_item):
        query_part, key_part, value_part, reset_point, state_in, grad_mixed, grad_state = shard_item
        decay_mask, into_weight, out_weight, link_decay = decay_tables(decay_rate, reset_point, TOK_DEV)
        query_float = query_part.astype(jnp.float32)
        key_float = key_part.astype(jnp.float32)
        value_float = value_part.astype(jnp.float32)
        weights = (jnp.einsum('thd,shd->hts', query_float, key_float) * key_scale * decay_mask).astype(jnp.bfloat16)
        grad_low = grad_mixed.astype(jnp.bfloat16).astype(jnp.float32)
        grad_weights = (jnp.einsum('thd,shd->hts', grad_low, value_float) * decay_mask).astype(jnp.bfloat16).astype(jnp.float32)
        grad_query = jnp.einsum('hts,shd->thd', grad_weights, key_float) * key_scale
        grad_query = grad_query + jnp.einsum('the,hde->thd', grad_mixed, state_in, precision=lax.Precision.HIGHEST) * into_weight
        grad_key = jnp.einsum('hts,thd->shd', grad_weights, query_float) * key_scale
        grad_key = grad_key + key_scale * jnp.einsum('she,hde->shd', value_float, grad_state, precision=lax.Precision.HIGHEST) * out_weight
        grad_value = jnp.einsum('hts,thd->shd', weights.astype(jnp.float32), grad_low)
        grad_value = grad_value + key_scale * jnp.einsum('shd,hde->she', key_float * out_weight, grad_state, precision=lax.Precision.HIGHEST)
        return (grad_query.astype(jnp.bfloat16), grad_key.astype(jnp.bfloat16), grad_value.astype(jnp.bfloat16))

    def forward_step(carried, step_item):
        term_decay, local_state, is_first = step_item
        chain_state = jnp.where(is_first, 0.0, carried)
        return (term_decay[:, None, None] * chain_state + local_state, chain_state)

    def backward_step(carried, step_item):
        entry_grad, link_decay, is_first, extra_grad = step_item
        grad_state = carried + extra_grad
        grad_first = entry_grad + link_decay[:, None, None] * grad_state
        return (jnp.where(is_first, 0.0, grad_first), (grad_state, grad_first))

    def group_pass(group_item):
        query_part, key_part, value_part, gate_part, grad_part, offsets, pairs = group_item
        resets = jnp.concatenate([jnp.full((quarter,), TOK_DEV, jnp.int32), offsets.astype(jnp.int32), jnp.full((N_CONTEXT - quarter - PROMPT_SHARDS,), TOK_DEV, jnp.int32)])
        owner_shards = (pairs + quarter).astype(jnp.int32)
        states, link_decays = lax.map(shard_state, (key_part, value_part, resets))
        term_decays = jnp.where(first_flags[:, None], 0.0, link_decays)
        zero_state = jnp.zeros(state_shape, jnp.float32)
        _, chains = lax.scan(forward_step, zero_state, (term_decays, states, first_flags))
        end_states = term_decays[:, :, None, None] * chains + states
        seed_states = end_states[owner_shards]
        seed_each = seed_states[jnp.maximum(pair_index, 0).astype(jnp.int32)]
        states_in = chains + seed_lift[:, :, None, None] * seed_each
        retained, grad_mixed, grad_gate, gain_parts, entries = lax.map(shard_forward, (query_part, key_part, value_part, gate_part, grad_part, resets, states_in))
        _, (unused_grads, grad_firsts) = lax.scan(backward_step, zero_state, (entries, link_decays, first_flags, jnp.zeros_like(entries)), reverse=True)
        picked = first_flags[:, None] & (pair_index[:, None] == pair_slots[None, :])
        seed_grads = lax.optimization_barrier(jnp.sum(jnp.where(picked[:, :, None, None, None], grad_firsts[:, None], 0.0), axis=0))
        owners = owner_shards[None, :] == shard_index[:, None]
        extras = lax.optimization_barrier(jnp.sum(jnp.where(owners[:, :, None, None, None], seed_grads[None], 0.0), axis=1))
        _, (grad_states, unused_firsts) = lax.scan(backward_step, zero_state, (entries, link_decays, first_flags, extras), reverse=True)
        grad_query, grad_key, grad_value = lax.map(shard_backward, (query_part, key_part, value_part, resets, states_in, grad_mixed, grad_states))
        return (retained, grad_query, grad_key, grad_value, grad_gate, lax.optimization_barrier(jnp.sum(gain_parts, axis=0)))
    group_results = lax.map(group_pass, (queries.reshape(grid_shape), key_rows.reshape(grid_shape), value_rows.reshape(grid_shape), gate_rows.reshape(grid_shape), out_grad.reshape(grid_shape), reset_offsets, pair_prompts))
    flat_shape = (TOKENS, CH)
    grad_gain = lax.optimization_barrier(jnp.sum(group_results[5], axis=0)).reshape(CH) / TOKENS ** 0.5
    return (group_results[0].reshape(flat_shape), group_results[1].reshape(flat_shape), group_results[2].reshape(flat_shape), group_results[3].reshape(flat_shape), group_results[4].reshape(flat_shape), grad_gain)
```

```python
import functools

import jax
import jax.numpy as jnp
from jax import lax
from jax.experimental import pallas as pl
from jax.experimental.pallas import tpu as pltpu
from jax.sharding import PartitionSpec as P

MESH = pl.DeviceIdType.MESH
F32 = jnp.float32
BF16 = jnp.bfloat16

ROW = 8
ROWS = 4
HD = 256
TOK = 128
SL = HD // ROW
SPAN = 4


def dot(a, b, ca, cb):
    return lax.dot_general(a, b, (((ca,), (cb,)), ((), ())), preferred_element_type=F32)


def split(x):
    hi = x.astype(BF16)
    return hi, (x - hi.astype(F32)).astype(BF16)


def remote(src, dst, send_sem, recv_sem, **where):
    return pltpu.make_async_remote_copy(
        src_ref=src,
        dst_ref=dst,
        send_sem=send_sem,
        recv_sem=recv_sem,
        device_id=where,
        device_id_type=MESH,
    )


def kernel(
    heads,
    n_dp,
    rate,
    resets,
    pairs,
    q_ref,
    k_ref,
    v_ref,
    g_ref,
    do_ref,
    gain_ref,
    ret_ref,
    dq_ref,
    dk_ref,
    dv_ref,
    dgate_ref,
    dgain_ref,
    l_buf,
    r1,
    o2,
    s_buf,
    e_buf,
    r3,
    o4,
    g_buf,
    t_out,
    t_in,
    c_out,
    c_in,
    b_out,
    b_in,
    dkp,
    dvp,
    gp,
    gz,
    gx_out,
    gx,
    gd_out,
    gd,
    ss,
    rs,
    xs,
    xr,
    gs,
    gr,
):
    me = lax.axis_index("context")
    my_dp = lax.axis_index("dp")
    x, z = me // ROW, lax.rem(me, ROW)
    is_prompt = jnp.logical_and(x >= 1, x <= 2)
    scale = HD**-0.5

    def ctx(xx, zz):
        return xx * ROW + lax.rem(zz + 2 * ROW, ROW)

    barrier = pltpu.get_barrier_semaphore()

    def greet_z(k, c):
        pl.semaphore_signal(
            barrier, inc=1, device_id={"context": ctx(x, z + k)}, device_id_type=MESH
        )
        return c

    def greet_x(k, c):
        pl.semaphore_signal(
            barrier, inc=1, device_id={"context": ctx(lax.rem(x + k, ROWS), z)}, device_id_type=MESH
        )
        return c

    def greet_dp(k, c):
        pl.semaphore_signal(
            barrier, inc=1, device_id={"dp": lax.rem(my_dp + k, n_dp)}, device_id_type=MESH
        )
        return c

    lax.fori_loop(1, ROW, greet_z, 0)
    lax.fori_loop(1, ROWS, greet_x, 0)
    lax.fori_loop(1, n_dp, greet_dp, 0)
    pl.semaphore_wait(barrier, ROW - 1 + ROWS - 1 + n_dp - 1)

    prompt_index = jnp.clip(me - ROW, 0, 2 * ROW - 1)
    rho = jnp.where(is_prompt, resets[0, prompt_index], TOK)

    def cols(h):
        return pl.ds(pl.multiple_of(h * HD, HD), HD)

    def column_weights(h):
        lam = rate[h]
        t = lax.broadcasted_iota(jnp.int32, (TOK, 1), 0)
        tf = t.astype(F32)
        into = jnp.where(t < rho, jnp.exp(-lam * (tf + 1.0)), 0.0)
        out = jnp.where(t >= lax.rem(rho, TOK), jnp.exp(-lam * (TOK - 1.0 - tf)), 0.0)
        return into, out

    def own_rows(zz):
        return pl.ds(pl.multiple_of(zz * SL, SL), SL)

    def to_owners(src, dst, phase, h):
        def one(k, c):
            zz = lax.rem(z + k, ROW)
            remote(
                src.at[h, own_rows(zz)],
                dst.at[h, k],
                ss.at[phase, h],
                rs.at[phase, h],
                context=x * ROW + zz,
            ).start()
            return c

        lax.fori_loop(1, ROW, one, 0)
        dst[h, 0] = src[h, own_rows(z)]

    def from_owner(src, dst, phase, h):
        def one(k, c):
            remote(
                src.at[h, k],
                dst.at[h, own_rows(z)],
                ss.at[phase, h],
                rs.at[phase, h],
                context=ctx(x, z - k),
            ).start()
            return c

        lax.fori_loop(1, ROW, one, 0)
        dst[h, own_rows(z)] = src[h, 0]

    def wait_row(buf, phase, h, send):
        ref = buf.at[h, pl.ds(1, ROW - 1)]
        c = remote(ref, ref, ss.at[phase, h], rs.at[phase, h], context=ctx(x, z + 1))
        if send:
            c.wait_send()
        else:
            c.wait_recv()

    def wait_full(buf, phase, h):
        ref = buf.at[h, pl.ds(0, HD - SL)]
        remote(ref, ref, ss.at[phase, h], rs.at[phase, h], context=ctx(x, z + 1)).wait_recv()

    def stage_a(h, c):
        _, out = column_weights(h)
        kw = k_ref[:, cols(h)].astype(F32) * (out * scale)
        hi, lo = split(kw)
        vh = v_ref[:, cols(h)]
        l_buf[h] = dot(hi, vh, 0, 0) + dot(lo, vh, 0, 0)
        to_owners(l_buf, r1, 0, h)
        return c

    lax.fori_loop(0, heads, stage_a, 0)

    def decay_row(h):
        return jnp.exp(jnp.full((1, HD), -float(TOK) * rate[h], F32))

    def link(h, j, row):
        return row * (resets[0, j] == TOK).astype(F32)

    def x_send(src, dst, kind, h, xx):
        return remote(src, dst, xs.at[kind, h], xr.at[kind, h], context=ctx(xx, z))

    def forward_prompt(h, first, start):
        row = decay_row(h)

        def step(jz, carry):
            s, c0, c1 = carry
            j = first + jz
            slot = lax.rem(z - jz + ROW, ROW)
            o2[h, slot] = s
            s = s * link(h, j, row) + r1[h, slot]
            c0 = c0 + s * (pairs[0, 0] == j).astype(F32)
            c1 = c1 + s * (pairs[0, 1] == j).astype(F32)
            return s, c0, c1

        zero = jnp.zeros((SL, HD), F32)
        s, c0, c1 = lax.fori_loop(0, ROW, step, (start, zero, zero))
        c_out[h, 0] = c0
        c_out[h, 1] = c1
        return s

    def stage_b(h, c):
        wait_row(r1, 0, h, False)

        @pl.when(x == 1)
        def _():
            t_out[h] = forward_prompt(h, 0, jnp.zeros((SL, HD), F32))
            x_send(t_out.at[h], t_in.at[h], 0, h, 2).start()
            x_send(c_out.at[h, 0], c_in.at[h, 0], 1, h, 0).start()
            x_send(c_out.at[h, 1], c_in.at[h, 0], 1, h, 3).start()

        @pl.when(x == 2)
        def _():
            x_send(t_out.at[h], t_in.at[h], 0, h, 2).wait_recv()
            forward_prompt(h, ROW, t_in[h])
            x_send(c_out.at[h, 0], c_in.at[h, 1], 1, h, 0).start()
            x_send(c_out.at[h, 1], c_in.at[h, 1], 1, h, 3).start()

        @pl.when(jnp.logical_not(is_prompt))
        def _():
            x_send(c_out.at[h], c_in.at[h], 1, h, 1).wait_recv()
            row = decay_row(h)

            def side(sd, cc):
                def step(m, s):
                    slot = lax.rem(z - sd * SPAN - m + ROW, ROW)
                    o2[h, slot] = s
                    return s * row + r1[h, slot]

                lax.fori_loop(0, SPAN, step, c_in[h, 0] + c_in[h, 1])
                return cc

            lax.fori_loop(0, ROW // SPAN, side, 0)

        from_owner(o2, s_buf, 1, h)
        return c

    lax.fori_loop(0, heads, stage_b, 0)

    gp[...] = jnp.zeros_like(gp)

    def stage_c(h, c):
        lam = rate[h]
        into, out = column_weights(h)
        ti = lax.broadcasted_iota(jnp.int32, (TOK, TOK), 0)
        si = lax.broadcasted_iota(jnp.int32, (TOK, TOK), 1)
        dist = (ti - si).astype(F32)
        allowed = (ti >= si) & ((ti >= rho) == (si >= rho))
        mask = jnp.where(allowed, jnp.exp(-lam * jnp.maximum(dist, 0.0)), 0.0)
        qh, kh, vh = q_ref[:, cols(h)], k_ref[:, cols(h)], v_ref[:, cols(h)]
        weights = (dot(qh, kh, 1, 1) * scale * mask).astype(BF16)
        mixed = dot(weights, vh, 1, 0)
        wait_full(s_buf, 1, h)
        s_hi, s_lo = split(s_buf[h])
        mixed = mixed + into * (dot(qh, s_hi, 1, 0) + dot(qh, s_lo, 1, 0))
        centre = mixed - jnp.mean(mixed, axis=1, keepdims=True)
        r = lax.rsqrt(jnp.mean(centre * centre, axis=1, keepdims=True) + 1e-05)
        xhat = centre * r
        gain = gain_ref[:, cols(h)]
        gate = g_ref[:, cols(h)].astype(F32)
        go = do_ref[:, cols(h)].astype(F32)
        sig = 1.0 / (1.0 + jnp.exp(-gate))
        silu = gate * sig
        ret_ref[:, cols(h)] = (silu * xhat * gain).astype(BF16)
        gox = go * xhat
        dgate_ref[:, cols(h)] = (gox * gain * (sig + silu * (1.0 - sig))).astype(BF16)
        gp[pl.ds(h, 1), :] = jnp.sum(gox * silu, axis=0, keepdims=True)
        dx = go * silu * gain
        dx = dx - jnp.mean(dx, axis=1, keepdims=True) - xhat * jnp.mean(
            dx * xhat, axis=1, keepdims=True
        )
        gm = dx * r
        e_hi, e_lo = split(gm * into)
        e_buf[h] = dot(qh, e_hi, 0, 0) + dot(qh, e_lo, 0, 0)
        to_owners(e_buf, r3, 2, h)
        low, rest = split(gm)
        gw = (dot(low, vh, 1, 1) * mask).astype(BF16)
        inter = dot(low, s_hi, 1, 1) + dot(low, s_lo, 1, 1) + dot(rest, s_hi, 1, 1)
        dq_ref[:, cols(h)] = (dot(gw, kh, 1, 0) * scale + inter * into).astype(BF16)
        dkp[h] = dot(gw, qh, 0, 0) * scale
        dvp[h] = dot(weights, low, 0, 0)
        return c

    lax.fori_loop(0, heads, stage_c, 0)

    def gain_z(k, c):
        remote(gp, gz.at[z], gs.at[0], gr.at[0], context=ctx(x, z + k)).start()
        return c

    lax.fori_loop(1, ROW, gain_z, 0)
    gz[z] = gp[...]

    def backward_prompt(h, first, start):
        row = decay_row(h)

        def step(i, g):
            jz = ROW - 1 - i
            j = first + jz
            slot = lax.rem(z - jz + ROW, ROW)
            g = g + b_in[h, 0] * (pairs[0, 0] == j).astype(F32)
            g = g + b_in[h, 1] * (pairs[0, 1] == j).astype(F32)
            o4[h, slot] = g
            return r3[h, slot] + g * link(h, j, row)

        return lax.fori_loop(0, ROW, step, start)

    def stage_d(h, c):
        wait_row(r3, 2, h, False)

        @pl.when(jnp.logical_not(is_prompt))
        def _():
            row = decay_row(h)

            def side(sd, total):
                def step(i, g):
                    slot = lax.rem(z - sd * SPAN - (SPAN - 1 - i) + ROW, ROW)
                    o4[h, slot] = g
                    return r3[h, slot] + g * row

                return total + lax.fori_loop(0, SPAN, step, jnp.zeros((SL, HD), F32))

            b_out[h] = lax.fori_loop(0, ROW // SPAN, side, jnp.zeros((SL, HD), F32))
            pair = x // 3
            x_send(b_out.at[h], b_in.at[h, pair], 3, h, 2).start()
            x_send(b_out.at[h], b_in.at[h, pair], 3, h, 1).start()

        @pl.when(is_prompt)
        def _():
            x_send(c_out.at[h], b_in.at[h], 3, h, 0).wait_recv()

        @pl.when(x == 2)
        def _():
            t_out[h] = backward_prompt(h, ROW, jnp.zeros((SL, HD), F32))
            x_send(t_out.at[h], t_in.at[h], 2, h, 1).start()

        @pl.when(x == 1)
        def _():
            x_send(t_out.at[h], t_in.at[h], 2, h, 2).wait_recv()
            backward_prompt(h, 0, t_in[h])

        from_owner(o4, g_buf, 3, h)
        return c

    lax.fori_loop(0, heads, stage_d, 0)

    w = gz.at[pl.ds(0, ROW - 1)]
    remote(w, w, gs.at[0], gr.at[0], context=ctx(x, z + 1)).wait()

    gx_out[...] = lax.fori_loop(1, ROW, lambda i, a: a + gz[i], gz[0])

    def gain_x(k, c):
        remote(
            gx_out, gx.at[x], gs.at[1], gr.at[1], context=ctx(lax.rem(x + k, ROWS), z)
        ).start()
        return c

    lax.fori_loop(1, ROWS, gain_x, 0)
    gx[x] = gx_out[...]

    def gain_dp(k, c):
        remote(gd_out, gd.at[my_dp], gs.at[2], gr.at[2], dp=lax.rem(my_dp + k, n_dp)).start()
        return c

    def stage_e(h, c):
        wait_full(g_buf, 3, h)
        _, out = column_weights(h)
        out = out * scale
        g_hi, g_lo = split(g_buf[h])
        kh, vh = k_ref[:, cols(h)], v_ref[:, cols(h)]
        dk_ref[:, cols(h)] = (
            dkp[h] + out * (dot(vh, g_hi, 1, 1) + dot(vh, g_lo, 1, 1))
        ).astype(BF16)
        dv_ref[:, cols(h)] = (
            dvp[h] + out * (dot(kh, g_hi, 1, 0) + dot(kh, g_lo, 1, 0))
        ).astype(BF16)

        @pl.when(h == heads // 2)
        def _():
            w = gx.at[pl.ds(0, ROWS - 1)]
            remote(w, w, gs.at[1], gr.at[1], context=ctx(x, z + 1)).wait()
            gd_out[...] = gx[0] + gx[1] + gx[2] + gx[3]
            lax.fori_loop(1, n_dp, gain_dp, 0)
            gd[my_dp] = gd_out[...]

        return c

    lax.fori_loop(0, heads, stage_e, 0)

    w = gd.at[pl.ds(0, n_dp - 1)]
    remote(w, w, gs.at[2], gr.at[2], context=ctx(x, z + 1)).wait()
    token_total = TOK * ROW * ROWS * n_dp
    dgain_ref[...] = lax.fori_loop(1, n_dp, lambda i, a: a + gd[i], gd[0]) * (token_total**-0.5)

    def drain(h, c):
        wait_row(r1, 0, h, True)
        wait_row(o2, 1, h, True)
        wait_row(r3, 2, h, True)
        wait_row(o4, 3, h, True)

        @pl.when(x == 1)
        def _():
            x_send(t_out.at[h], t_in.at[h], 0, h, 2).wait_send()

        @pl.when(x == 2)
        def _():
            x_send(t_out.at[h], t_in.at[h], 2, h, 1).wait_send()

        @pl.when(is_prompt)
        def _():
            x_send(c_out.at[h], c_in.at[h], 1, h, 0).wait_send()

        @pl.when(jnp.logical_not(is_prompt))
        def _():
            x_send(c_out.at[h], b_in.at[h], 3, h, 1).wait_send()

        return c

    lax.fori_loop(0, heads, drain, 0)


def solution(mesh):
    n_dp = mesh.shape["dp"]
    assert mesh.shape["context"] == ROW * ROWS

    def per_device(
        queries,
        key_rows,
        value_rows,
        gate_rows,
        out_grad,
        decay_rate,
        norm_gain,
        reset_offsets,
        pair_prompts,
    ):
        heads = decay_rate.shape[0]
        flat = jax.ShapeDtypeStruct(queries.shape, BF16)
        vmem = pl.BlockSpec(memory_space=pltpu.VMEM)
        smem = pl.BlockSpec(memory_space=pltpu.SMEM)
        state = pltpu.VMEM((heads, HD, HD), F32)
        slots = pltpu.VMEM((heads, ROW, SL, HD), F32)
        piece = pltpu.VMEM((heads, SL, HD), F32)
        two = pltpu.VMEM((heads, 2, SL, HD), F32)
        part = pltpu.VMEM((heads, TOK, HD), F32)
        small = pltpu.VMEM((8, HD), F32)
        dma = pltpu.SemaphoreType.DMA
        outs = pl.pallas_call(
            functools.partial(kernel, heads, n_dp),
            out_shape=(flat, flat, flat, flat, flat, jax.ShapeDtypeStruct((8, HD), F32)),
            in_specs=[smem] * 3 + [vmem] * 6,
            out_specs=(vmem,) * 6,
            scratch_shapes=[
                state,
                slots,
                slots,
                state,
                state,
                slots,
                slots,
                state,
                piece,
                piece,
                two,
                two,
                piece,
                two,
                part,
                part,
                small,
                pltpu.VMEM((ROW, 8, HD), F32),
                small,
                pltpu.VMEM((ROWS, 8, HD), F32),
                small,
                pltpu.VMEM((n_dp, 8, HD), F32),
                dma((4, heads)),
                dma((4, heads)),
                dma((4, heads)),
                dma((4, heads)),
                dma((3,)),
                dma((3,)),
            ],
            compiler_params=pltpu.CompilerParams(
                collective_id=0, has_side_effects=True, vmem_limit_bytes=40 << 20
            ),
        )(
            decay_rate,
            reset_offsets,
            pair_prompts,
            queries,
            key_rows,
            value_rows,
            gate_rows,
            out_grad,
            norm_gain.reshape(1, -1),
        )
        return outs[:5] + (outs[5][:heads].reshape(-1),)

    rows = P(("dp", "context"), "tensor")
    in_specs = (rows,) * 5 + (P("tensor"), P("tensor"), P("dp", None), P("dp", None))
    return jax.shard_map(
        per_device,
        mesh=mesh,
        in_specs=in_specs,
        out_specs=(rows,) * 5 + (P("tensor"),),
        check_vma=False,
    )
```

```python
import functools

import jax
import jax.numpy as jnp
from jax import lax
from jax.experimental import pallas as pl
from jax.experimental.pallas import tpu as pltpu
from jax.sharding import PartitionSpec as P

MESH = pl.DeviceIdType.MESH
F32 = jnp.float32
BF16 = jnp.bfloat16

ROW = 8
ROWS = 4
HD = 256
TOK = 128
SPAN = 4
PROMPTS = 16
OWNERS = 16
SL = HD // OWNERS
PARTS = 4
PR = HD // PARTS


def dot(a, b, ca, cb):
    return lax.dot_general(a, b, (((ca,), (cb,)), ((), ())), preferred_element_type=F32)


def split(x):
    hi = x.astype(BF16)
    return hi, (x - hi.astype(F32)).astype(BF16)


def remote(src, dst, send_sem, recv_sem, **where):
    return pltpu.make_async_remote_copy(
        src_ref=src,
        dst_ref=dst,
        send_sem=send_sem,
        recv_sem=recv_sem,
        device_id=where,
        device_id_type=MESH,
    )


def kernel(
    heads,
    n_dp,
    rate,
    resets,
    pairs,
    gain_ref,
    q_hbm,
    k_hbm,
    v_hbm,
    g_hbm,
    do_hbm,
    ret_hbm,
    dq_hbm,
    dk_hbm,
    dv_hbm,
    dgate_hbm,
    dgain_ref,
    q_ref,
    k_ref,
    v_ref,
    g_ref,
    do_ref,
    ret_ref,
    dq_ref,
    dk_ref,
    dv_ref,
    dgate_ref,
    l_buf,
    s_buf,
    eo_buf,
    e_buf,
    n_buf,
    no_buf,
    x_buf,
    r1,
    o2,
    r3,
    o4,
    dkp,
    dvp,
    gp,
    gz,
    gx_out,
    gx,
    gd_out,
    gd,
    ss,
    rs,
    cs,
    cr,
    bs,
    br,
    gs,
    gr,
    in_sem,
    out_sem,
):
    me = lax.axis_index("context")
    my_dp = lax.axis_index("dp")
    x, z = me // ROW, lax.rem(me, ROW)
    m = lax.rem(z, SPAN)
    block = me // SPAN
    is_prompt = jnp.logical_and(x >= 1, x <= 2)
    is_owner = jnp.logical_not(is_prompt)
    w = jnp.where(x == ROWS - 1, ROW, 0) + z
    prompt_index = jnp.clip(me - ROW, 0, PROMPTS - 1)
    first_prompt = jnp.logical_and(is_prompt, m == 0)
    first_response = jnp.logical_and(is_owner, m == 0)
    start_of_all = me == ROW
    scale = HD**-0.5

    loads = [
        pltpu.make_async_copy(src, dst, in_sem.at[i])
        for i, (src, dst) in enumerate(
            ((k_hbm, k_ref), (v_hbm, v_ref), (q_hbm, q_ref), (g_hbm, g_ref), (do_hbm, do_ref))
        )
    ]
    for load in loads:
        load.start()

    n_context = ROW * ROWS
    barrier = pltpu.get_barrier_semaphore()

    def greet(k, c):
        pl.semaphore_signal(
            barrier,
            inc=1,
            device_id={"context": lax.rem(me + k, n_context)},
            device_id_type=MESH,
        )
        return c

    def greet_dp(k, c):
        pl.semaphore_signal(
            barrier, inc=1, device_id={"dp": lax.rem(my_dp + k, n_dp)}, device_id_type=MESH
        )
        return c

    lax.fori_loop(1, n_context, greet, 0)
    lax.fori_loop(1, n_dp, greet_dp, 0)
    pl.semaphore_wait(barrier, n_context - 1 + n_dp - 1)

    rho = jnp.where(is_prompt, resets[0, prompt_index], TOK)

    def cols(h):
        return pl.ds(pl.multiple_of(h * HD, HD), HD)

    def column_weights(h):
        lam = rate[h]
        t = lax.broadcasted_iota(jnp.int32, (TOK, 1), 0)
        tf = t.astype(F32)
        into = jnp.where(t < rho, jnp.exp(-lam * (tf + 1.0)), 0.0)
        out = jnp.where(t >= lax.rem(rho, TOK), jnp.exp(-lam * (TOK - 1.0 - tf)), 0.0)
        return into, out

    def decay_row(h):
        return jnp.exp(jnp.full((1, HD), -float(TOK) * rate[h], F32))

    def link(h, j, row):
        return row * (resets[0, j] == TOK).astype(F32)

    def my_link(h):
        return decay_row(h) * (rho == TOK).astype(F32)

    def slice_of(ww):
        return pl.ds(pl.multiple_of(ww * SL, SL), SL)

    def part(p):
        return pl.ds(pl.multiple_of(p * PR, PR), PR)

    def owner_ctx(ww):
        return (ww // ROW) * ((ROWS - 1) * ROW) + lax.rem(ww, ROW)

    def any_wait(ref, sems, phase, h):
        return remote(ref, ref, ss.at[phase, h], sems.at[phase, h], context=owner_ctx(0))

    def stage_a(h, c):
        _, out = column_weights(h)
        kw = k_ref[:, cols(h)].astype(F32) * (out * scale)
        hi, lo = split(kw)
        vh = v_ref[:, cols(h)]
        l_buf[h] = dot(hi, vh, 0, 0) + dot(lo, vh, 0, 0)

        @pl.when(is_prompt)
        def _():
            def one(k, cc):
                ww = lax.rem(k, 2) * ROW + lax.rem(z + k // 2, ROW)
                remote(
                    l_buf.at[h, slice_of(ww)],
                    r1.at[h, prompt_index],
                    ss.at[0, h],
                    rs.at[0, h],
                    context=owner_ctx(ww),
                ).start()
                return cc

            lax.fori_loop(0, OWNERS, one, 0)

        return c

    loads[0].wait()
    loads[1].wait()
    lax.fori_loop(0, heads, stage_a, 0)

    def stage_b(h):
        any_wait(r1.at[h], rs, 0, h).wait_recv()
        row = decay_row(h)

        def per_block(b, carry):
            o2[h, b] = carry[0]

            def step(mm, inner):
                s, c0, c1 = inner
                j = b * SPAN + mm
                s = s * link(h, j, row) + r1[h, j]
                c0 = c0 + s * (pairs[0, 0] == j).astype(F32)
                c1 = c1 + s * (pairs[0, 1] == j).astype(F32)
                return s, c0, c1

            return lax.fori_loop(0, SPAN, step, carry)

        zero = jnp.zeros((SL, HD), F32)
        _, c0, c1 = lax.fori_loop(0, PROMPTS // SPAN, per_block, (zero, zero, zero))
        o2[h, 4] = c0
        o2[h, 5] = c1

        def to_prompt(b, c):
            remote(
                o2.at[h, b],
                s_buf.at[h, slice_of(w)],
                ss.at[1, h],
                rs.at[1, h],
                context=ROW + b * SPAN,
            ).start()
            return c

        lax.fori_loop(1, PROMPTS // SPAN, to_prompt, 0)

        def to_response(k, c):
            target = (k // 2) * ((ROWS - 1) * ROW) + lax.rem(k, 2) * SPAN

            @pl.when(target != me)
            def _():
                remote(
                    o2.at[h, 4 + k // 2],
                    s_buf.at[h, slice_of(w)],
                    ss.at[1, h],
                    rs.at[1, h],
                    context=target,
                ).start()

            @pl.when(target == me)
            def _():
                s_buf[h, slice_of(w), :] = o2[h, 4 + k // 2]

            return c

        lax.fori_loop(0, 4, to_response, 0)

    def chain(h):
        @pl.when(start_of_all)
        def _():
            s_buf[h] = jnp.zeros((HD, HD), F32)

        @pl.when(jnp.logical_and(first_prompt, jnp.logical_not(start_of_all)))
        def _():
            any_wait(s_buf.at[h], rs, 1, h).wait_recv()

        @pl.when(first_response)
        def _():
            any_wait(s_buf.at[h, pl.ds(0, HD - SL)], rs, 1, h).wait_recv()

        factor = my_link(h)

        def step(p, c):
            here = s_buf.at[h, part(p)]

            @pl.when(m > 0)
            def _():
                remote(here, here, cs.at[h, p], cr.at[h, p], context=me).wait_recv()

            @pl.when(m < SPAN - 1)
            def _():
                eo_buf[h, part(p), :] = s_buf[h, part(p), :] * factor + l_buf[h, part(p), :]
                remote(
                    eo_buf.at[h, part(p)], here, cs.at[h, p], cr.at[h, p], context=me + 1
                ).start()

            return c

        lax.fori_loop(0, PARTS, step, 0)

    def store(src, dst, kind, h):
        pltpu.make_async_copy(src.at[:, cols(h)], dst.at[:, cols(h)], out_sem.at[kind]).start()

    def stage_c(h):
        lam = rate[h]
        into, out = column_weights(h)
        ti = lax.broadcasted_iota(jnp.int32, (TOK, TOK), 0)
        si = lax.broadcasted_iota(jnp.int32, (TOK, TOK), 1)
        dist = (ti - si).astype(F32)
        allowed = (ti >= si) & ((ti >= rho) == (si >= rho))
        mask = jnp.where(allowed, jnp.exp(-lam * jnp.maximum(dist, 0.0)), 0.0)
        qh, kh, vh = q_ref[:, cols(h)], k_ref[:, cols(h)], v_ref[:, cols(h)]
        weights = (dot(qh, kh, 1, 1) * scale * mask).astype(BF16)
        mixed = dot(weights, vh, 1, 0)
        s_hi, s_lo = split(s_buf[h])
        mixed = mixed + into * (dot(qh, s_hi, 1, 0) + dot(qh, s_lo, 1, 0))
        centre = mixed - jnp.mean(mixed, axis=1, keepdims=True)
        r = lax.rsqrt(jnp.mean(centre * centre, axis=1, keepdims=True) + 1e-05)
        xhat = centre * r
        gain = gain_ref[:, cols(h)]
        gate = g_ref[:, cols(h)].astype(F32)
        go = do_ref[:, cols(h)].astype(F32)
        sig = 1.0 / (1.0 + jnp.exp(-gate))
        silu = gate * sig
        ret_ref[:, cols(h)] = (silu * xhat * gain).astype(BF16)
        gox = go * xhat
        dgate_ref[:, cols(h)] = (gox * gain * (sig + silu * (1.0 - sig))).astype(BF16)
        gp[pl.ds(h, 1), :] = jnp.sum(gox * silu, axis=0, keepdims=True)
        dx = go * silu * gain
        dx = dx - jnp.mean(dx, axis=1, keepdims=True) - xhat * jnp.mean(
            dx * xhat, axis=1, keepdims=True
        )
        gm = dx * r
        e_hi, e_lo = split(gm * into)
        e_buf[h] = dot(qh, e_hi, 0, 0) + dot(qh, e_lo, 0, 0)
        low, rest = split(gm)
        gw = (dot(low, vh, 1, 1) * mask).astype(BF16)
        inter = dot(low, s_hi, 1, 1) + dot(low, s_lo, 1, 1) + dot(rest, s_hi, 1, 1)
        dq_ref[:, cols(h)] = (dot(gw, kh, 1, 0) * scale + inter * into).astype(BF16)
        dkp[h] = dot(gw, qh, 0, 0) * scale
        dvp[h] = dot(weights, low, 0, 0)
        store(ret_ref, ret_hbm, 0, h)
        store(dq_ref, dq_hbm, 1, h)
        store(dgate_ref, dgate_hbm, 4, h)

    def backward(h):
        @pl.when(m == SPAN - 1)
        def _():
            n_buf[h] = jnp.zeros((HD, HD), F32)

        factor = my_link(h)
        slot = jnp.where(is_prompt, block + 1, jnp.where(block < 2, block, block - 4))

        def step(p, c):
            here = n_buf.at[h, part(p)]

            @pl.when(m < SPAN - 1)
            def _():
                remote(here, here, bs.at[h, p], br.at[h, p], context=me).wait_recv()

            no_buf[h, part(p), :] = e_buf[h, part(p), :] + n_buf[h, part(p), :] * factor

            @pl.when(m > 0)
            def _():
                remote(
                    no_buf.at[h, part(p)], here, bs.at[h, p], br.at[h, p], context=me - 1
                ).start()

            @pl.when(jnp.logical_and(m == 0, jnp.logical_not(start_of_all)))
            def _():
                def one(k, cc):
                    ww = p * (OWNERS // PARTS) + k
                    target = owner_ctx(ww)

                    @pl.when(target != me)
                    def _():
                        remote(
                            no_buf.at[h, slice_of(ww)],
                            r3.at[h, slot],
                            ss.at[2, h],
                            rs.at[2, h],
                            context=target,
                        ).start()

                    @pl.when(target == me)
                    def _():
                        r3[h, slot] = no_buf[h, slice_of(ww), :]

                    return cc

                lax.fori_loop(0, OWNERS // PARTS, one, 0)

            return c

        lax.fori_loop(0, PARTS, step, 0)

    def stage_d(h):
        @pl.when(m == 0)
        def _():
            any_wait(r3.at[h, pl.ds(0, 6)], rs, 2, h).wait_recv()

        @pl.when(m > 0)
        def _():
            any_wait(r3.at[h], rs, 2, h).wait_recv()

        row = decay_row(h)
        s0 = r3[h, 0] + r3[h, 1]
        s1 = r3[h, 2] + r3[h, 3]

        def run(b, g):
            def step(i, g):
                j = b * SPAN + SPAN - 1 - i
                g = g + s0 * (pairs[0, 0] == j).astype(F32)
                g = g + s1 * (pairs[0, 1] == j).astype(F32)
                o4[h, j] = g
                return g * link(h, j, row)

            return lax.fori_loop(0, SPAN, step, g)

        def per_block(i, g):
            b = PROMPTS // SPAN - 1 - i
            return run(b, g) + r3[h, b + 3]

        g = lax.fori_loop(0, PROMPTS // SPAN - 1, per_block, jnp.zeros((SL, HD), F32))
        run(0, g)

        def one(k, c):
            j = lax.rem(k, 2) * ROW + lax.rem(z + k // 2, ROW)
            remote(
                o4.at[h, j],
                x_buf.at[h, slice_of(w)],
                ss.at[3, h],
                rs.at[3, h],
                context=ROW + j,
            ).start()
            return c

        lax.fori_loop(0, PROMPTS, one, 0)

    gp[...] = jnp.zeros_like(gp)

    def gain_row_send():
        def one(k, c):
            remote(
                gp, gz.at[z], gs.at[0], gr.at[0], context=x * ROW + lax.rem(z + k, ROW)
            ).start()
            return c

        lax.fori_loop(1, ROW, one, 0)
        gz[z] = gp[...]

    def gain_x_send():
        ref = gz.at[pl.ds(0, ROW - 1)]
        remote(ref, ref, gs.at[0], gr.at[0], context=me).wait()
        gx_out[...] = lax.fori_loop(1, ROW, lambda i, a: a + gz[i], gz[0])

        def one(k, c):
            remote(
                gx_out, gx.at[x], gs.at[1], gr.at[1], context=lax.rem(x + k, ROWS) * ROW + z
            ).start()
            return c

        lax.fori_loop(1, ROWS, one, 0)
        gx[x] = gx_out[...]

    def gain_dp_send():
        ref = gx.at[pl.ds(0, ROWS - 1)]
        remote(ref, ref, gs.at[1], gr.at[1], context=me).wait()
        gd_out[...] = lax.fori_loop(1, ROWS, lambda i, a: a + gx[i], gx[0])

        def one(k, c):
            remote(
                gd_out, gd.at[my_dp], gs.at[2], gr.at[2], dp=lax.rem(my_dp + k, n_dp)
            ).start()
            return c

        lax.fori_loop(1, n_dp, one, 0)
        gd[my_dp] = gd_out[...]

    for load in loads[2:]:
        load.wait()

    lag = is_owner.astype(jnp.int32)

    def valid(h):
        return jnp.logical_and(h >= 0, h < heads)

    def beat(i, c):
        @pl.when(jnp.logical_and(is_owner, i < heads))
        def _():
            stage_b(i)

        hc = i - lag

        @pl.when(valid(hc))
        def _():
            chain(hc)
            stage_c(hc)

        hb = hc - (SPAN - 1) + m

        @pl.when(valid(hb))
        def _():
            backward(hb)

        hd = i - 5

        @pl.when(jnp.logical_and(is_owner, valid(hd)))
        def _():
            stage_d(hd)

        @pl.when(hc == heads)
        def _():
            gain_row_send()

        @pl.when(i == heads + 2)
        def _():
            gain_x_send()

        return c

    lax.fori_loop(0, heads + 5, beat, 0)

    def stage_e(h, c):
        @pl.when(is_prompt)
        def _():
            any_wait(x_buf.at[h], rs, 3, h).wait_recv()
            n_buf[h] = n_buf[h] + x_buf[h]

        _, out = column_weights(h)
        out = out * scale
        g_hi, g_lo = split(n_buf[h])
        kh, vh = k_ref[:, cols(h)], v_ref[:, cols(h)]
        dk_ref[:, cols(h)] = (
            dkp[h] + out * (dot(vh, g_hi, 1, 1) + dot(vh, g_lo, 1, 1))
        ).astype(BF16)
        dv_ref[:, cols(h)] = (
            dvp[h] + out * (dot(kh, g_hi, 1, 0) + dot(kh, g_lo, 1, 0))
        ).astype(BF16)
        store(dk_ref, dk_hbm, 2, h)
        store(dv_ref, dv_hbm, 3, h)

        @pl.when(h == 1)
        def _():
            gain_dp_send()

        return c

    lax.fori_loop(0, heads, stage_e, 0)

    ref = gd.at[pl.ds(0, n_dp - 1)]
    remote(ref, ref, gs.at[2], gr.at[2], context=me).wait()
    token_total = TOK * n_context * n_dp
    dgain_ref[...] = lax.fori_loop(1, n_dp, lambda i, a: a + gd[i], gd[0]) * (token_total**-0.5)

    def drain(h, c):
        @pl.when(is_prompt)
        def _():
            any_wait(l_buf.at[h], rs, 0, h).wait_send()

        @pl.when(is_owner)
        def _():
            any_wait(o4.at[h], rs, 3, h).wait_send()

        @pl.when(jnp.logical_and(is_owner, m > 0))
        def _():
            any_wait(r1.at[h, pl.ds(0, 7)], rs, 1, h).wait_send()

        @pl.when(first_response)
        def _():
            any_wait(r1.at[h, pl.ds(0, 6)], rs, 1, h).wait_send()
            any_wait(no_buf.at[h, pl.ds(0, HD - SL)], rs, 2, h).wait_send()

        @pl.when(jnp.logical_and(first_prompt, jnp.logical_not(start_of_all)))
        def _():
            any_wait(no_buf.at[h], rs, 2, h).wait_send()

        def step(p, cc):
            ref = no_buf.at[h, part(p)]

            @pl.when(m < SPAN - 1)
            def _():
                remote(ref, ref, cs.at[h, p], cr.at[h, p], context=me).wait_send()

            @pl.when(m > 0)
            def _():
                remote(ref, ref, bs.at[h, p], br.at[h, p], context=me).wait_send()

            return cc

        lax.fori_loop(0, PARTS, step, 0)
        return c

    lax.fori_loop(0, heads, drain, 0)
    for i, (src, dst) in enumerate(
        (
            (ret_ref, ret_hbm),
            (dq_ref, dq_hbm),
            (dk_ref, dk_hbm),
            (dv_ref, dv_hbm),
            (dgate_ref, dgate_hbm),
        )
    ):
        pltpu.make_async_copy(src, dst, out_sem.at[i]).wait()


def solution(mesh):
    n_dp = mesh.shape["dp"]
    assert mesh.shape["context"] == ROW * ROWS

    def per_device(
        queries,
        key_rows,
        value_rows,
        gate_rows,
        out_grad,
        decay_rate,
        norm_gain,
        reset_offsets,
        pair_prompts,
    ):
        heads = decay_rate.shape[0]
        flat = jax.ShapeDtypeStruct(queries.shape, BF16)
        vmem = pl.BlockSpec(memory_space=pltpu.VMEM)
        smem = pl.BlockSpec(memory_space=pltpu.SMEM)
        hbm = pl.BlockSpec(memory_space=pltpu.HBM)
        state = pltpu.VMEM((heads, HD, HD), F32)
        held = pltpu.VMEM(queries.shape, BF16)
        part = pltpu.VMEM((heads, TOK, HD), F32)
        small = pltpu.VMEM((8, HD), F32)
        dma = pltpu.SemaphoreType.DMA
        outs = pl.pallas_call(
            functools.partial(kernel, heads, n_dp),
            out_shape=(flat,) * 5 + (jax.ShapeDtypeStruct((8, HD), F32),),
            in_specs=[smem] * 3 + [vmem] + [hbm] * 5,
            out_specs=(hbm,) * 5 + (vmem,),
            scratch_shapes=[held] * 10
            + [state] * 7
            + [pltpu.VMEM((heads, n, SL, HD), F32) for n in (PROMPTS, 6, 7, PROMPTS)]
            + [
                part,
                part,
                small,
                pltpu.VMEM((ROW, 8, HD), F32),
                small,
                pltpu.VMEM((ROWS, 8, HD), F32),
                small,
                pltpu.VMEM((n_dp, 8, HD), F32),
                dma((4, heads)),
                dma((4, heads)),
                dma((heads, PARTS)),
                dma((heads, PARTS)),
                dma((heads, PARTS)),
                dma((heads, PARTS)),
                dma((3,)),
                dma((3,)),
                dma((5,)),
                dma((5,)),
            ],
            compiler_params=pltpu.CompilerParams(
                collective_id=0, has_side_effects=True, vmem_limit_bytes=56 << 20
            ),
        )(
            decay_rate,
            reset_offsets,
            pair_prompts,
            norm_gain.reshape(1, -1),
            queries,
            key_rows,
            value_rows,
            gate_rows,
            out_grad,
        )
        return outs[:5] + (outs[5][:heads].reshape(-1),)

    rows = P(("dp", "context"), "tensor")
    in_specs = (rows,) * 5 + (P("tensor"), P("tensor"), P("dp", None), P("dp", None))
    return jax.shard_map(
        per_device,
        mesh=mesh,
        in_specs=in_specs,
        out_specs=(rows,) * 5 + (P("tensor"),),
        check_vma=False,
    )
```

```python
import functools

import jax
import jax.numpy as jnp
from jax import lax
from jax.experimental import pallas as pl
from jax.experimental.pallas import tpu as pltpu
from jax.sharding import PartitionSpec as P

MESH = pl.DeviceIdType.MESH
F32 = jnp.float32
BF16 = jnp.bfloat16

ROW = 8
ROWS = 4
HD = 256
TOK = 128
SL = HD // ROW
SPAN = 4


def dot(a, b, ca, cb):
    return lax.dot_general(a, b, (((ca,), (cb,)), ((), ())), preferred_element_type=F32)


def split(x):
    hi = x.astype(BF16)
    return hi, (x - hi.astype(F32)).astype(BF16)


def remote(src, dst, send_sem, recv_sem, **where):
    return pltpu.make_async_remote_copy(
        src_ref=src,
        dst_ref=dst,
        send_sem=send_sem,
        recv_sem=recv_sem,
        device_id=where,
        device_id_type=MESH,
    )


def kernel(
    heads,
    n_dp,
    rate,
    resets,
    pairs,
    q_hbm,
    k_hbm,
    v_hbm,
    g_hbm,
    do_hbm,
    gain_hbm,
    ret_hbm,
    dq_hbm,
    dk_hbm,
    dv_hbm,
    dgate_hbm,
    dgain_ref,
    q_ref,
    k_ref,
    v_ref,
    g_ref,
    do_ref,
    ret_ref,
    dq_ref,
    dk_ref,
    dv_ref,
    dgate_ref,
    gain_ref,
    l_buf,
    r1,
    o2,
    s_buf,
    e_buf,
    r3,
    o4,
    g_buf,
    t_out,
    t_in,
    c_out,
    c_in,
    b_out,
    b_in,
    dkp,
    dvp,
    gp,
    gz,
    gx_out,
    gx,
    gd_out,
    gd,
    ss,
    rs,
    xs,
    xr,
    gs,
    gr,
    in_sem,
    out_sem,
):
    me = lax.axis_index("context")
    my_dp = lax.axis_index("dp")
    x, z = me // ROW, lax.rem(me, ROW)
    is_prompt = jnp.logical_and(x >= 1, x <= 2)
    scale = HD**-0.5

    def ctx(xx, zz):
        return xx * ROW + lax.rem(zz + 2 * ROW, ROW)

    loads = [
        pltpu.make_async_copy(src, dst, in_sem.at[i])
        for i, (src, dst) in enumerate(
            (
                (k_hbm, k_ref),
                (v_hbm, v_ref),
                (q_hbm, q_ref),
                (g_hbm, g_ref),
                (do_hbm, do_ref),
                (gain_hbm, gain_ref),
            )
        )
    ]
    for load in loads:
        load.start()

    barrier = pltpu.get_barrier_semaphore()

    def greet_z(k, c):
        pl.semaphore_signal(
            barrier, inc=1, device_id={"context": ctx(x, z + k)}, device_id_type=MESH
        )
        return c

    def greet_x(k, c):
        pl.semaphore_signal(
            barrier, inc=1, device_id={"context": ctx(lax.rem(x + k, ROWS), z)}, device_id_type=MESH
        )
        return c

    def greet_dp(k, c):
        pl.semaphore_signal(
            barrier, inc=1, device_id={"dp": lax.rem(my_dp + k, n_dp)}, device_id_type=MESH
        )
        return c

    lax.fori_loop(1, ROW, greet_z, 0)
    lax.fori_loop(1, ROWS, greet_x, 0)
    lax.fori_loop(1, n_dp, greet_dp, 0)
    prompt_index = jnp.clip(me - ROW, 0, 2 * ROW - 1)
    rho = jnp.where(is_prompt, resets[0, prompt_index], TOK)

    def cols(h):
        return pl.ds(pl.multiple_of(h * HD, HD), HD)

    def column_weights(h):
        lam = rate[h]
        t = lax.broadcasted_iota(jnp.int32, (TOK, 1), 0)
        tf = t.astype(F32)
        into = jnp.where(t < rho, jnp.exp(-lam * (tf + 1.0)), 0.0)
        out = jnp.where(t >= lax.rem(rho, TOK), jnp.exp(-lam * (TOK - 1.0 - tf)), 0.0)
        return into, out

    def own_rows(zz):
        return pl.ds(pl.multiple_of(zz * SL, SL), SL)

    def to_owners(src, dst, phase, h):
        def one(k, c):
            zz = lax.rem(z + k, ROW)
            remote(
                src.at[h, own_rows(zz)],
                dst.at[h, k],
                ss.at[phase, h],
                rs.at[phase, h],
                context=x * ROW + zz,
            ).start()
            return c

        lax.fori_loop(1, ROW, one, 0)
        dst[h, 0] = src[h, own_rows(z)]

    def from_owner(src, dst, phase, h):
        def one(k, c):
            remote(
                src.at[h, k],
                dst.at[h, own_rows(z)],
                ss.at[phase, h],
                rs.at[phase, h],
                context=ctx(x, z - k),
            ).start()
            return c

        lax.fori_loop(1, ROW, one, 0)
        dst[h, own_rows(z)] = src[h, 0]

    def wait_row(buf, phase, h, send):
        ref = buf.at[h, pl.ds(1, ROW - 1)]
        c = remote(ref, ref, ss.at[phase, h], rs.at[phase, h], context=ctx(x, z + 1))
        if send:
            c.wait_send()
        else:
            c.wait_recv()

    def wait_full(buf, phase, h):
        ref = buf.at[h, pl.ds(0, HD - SL)]
        remote(ref, ref, ss.at[phase, h], rs.at[phase, h], context=ctx(x, z + 1)).wait_recv()

    def stage_a(h, c):
        _, out = column_weights(h)
        kw = k_ref[:, cols(h)].astype(F32) * (out * scale)
        hi, lo = split(kw)
        vh = v_ref[:, cols(h)]
        l_buf[h] = dot(hi, vh, 0, 0) + dot(lo, vh, 0, 0)
        return c

    loads[0].wait()
    loads[1].wait()
    lax.fori_loop(0, heads, stage_a, 0)
    pl.semaphore_wait(barrier, ROW - 1 + ROWS - 1 + n_dp - 1)

    def send_a(h, c):
        to_owners(l_buf, r1, 0, h)
        return c

    lax.fori_loop(0, heads, send_a, 0)

    def decay_row(h):
        return jnp.exp(jnp.full((1, HD), -float(TOK) * rate[h], F32))

    def link(h, j, row):
        return row * (resets[0, j] == TOK).astype(F32)

    def x_send(src, dst, kind, h, xx):
        return remote(src, dst, xs.at[kind, h], xr.at[kind, h], context=ctx(xx, z))

    def forward_prompt(h, first, start):
        row = decay_row(h)

        def step(jz, carry):
            s, c0, c1 = carry
            j = first + jz
            slot = lax.rem(z - jz + ROW, ROW)
            o2[h, slot] = s
            s = s * link(h, j, row) + r1[h, slot]
            c0 = c0 + s * (pairs[0, 0] == j).astype(F32)
            c1 = c1 + s * (pairs[0, 1] == j).astype(F32)
            return s, c0, c1

        zero = jnp.zeros((SL, HD), F32)
        s, c0, c1 = lax.fori_loop(0, ROW, step, (start, zero, zero))
        c_out[h, 0] = c0
        c_out[h, 1] = c1
        return s

    def stage_b(h, c):
        wait_row(r1, 0, h, False)

        @pl.when(x == 1)
        def _():
            t_out[h] = forward_prompt(h, 0, jnp.zeros((SL, HD), F32))
            x_send(t_out.at[h], t_in.at[h], 0, h, 2).start()
            x_send(c_out.at[h, 0], c_in.at[h, 0], 1, h, 0).start()
            x_send(c_out.at[h, 1], c_in.at[h, 0], 1, h, 3).start()

        @pl.when(x == 2)
        def _():
            x_send(t_out.at[h], t_in.at[h], 0, h, 2).wait_recv()
            forward_prompt(h, ROW, t_in[h])
            x_send(c_out.at[h, 0], c_in.at[h, 1], 1, h, 0).start()
            x_send(c_out.at[h, 1], c_in.at[h, 1], 1, h, 3).start()

        @pl.when(jnp.logical_not(is_prompt))
        def _():
            x_send(c_out.at[h], c_in.at[h], 1, h, 1).wait_recv()
            row = decay_row(h)

            def side(sd, cc):
                def step(m, s):
                    slot = lax.rem(z - sd * SPAN - m + ROW, ROW)
                    o2[h, slot] = s
                    return s * row + r1[h, slot]

                lax.fori_loop(0, SPAN, step, c_in[h, 0] + c_in[h, 1])
                return cc

            lax.fori_loop(0, ROW // SPAN, side, 0)

        from_owner(o2, s_buf, 1, h)
        return c

    lax.fori_loop(0, heads, stage_b, 0)

    gp[...] = jnp.zeros_like(gp)
    for load in loads[2:]:
        load.wait()

    results = (
        (ret_ref, ret_hbm),
        (dq_ref, dq_hbm),
        (dk_ref, dk_hbm),
        (dv_ref, dv_hbm),
        (dgate_ref, dgate_hbm),
    )

    def store(h, *kinds):
        for i in kinds:
            src, dst = results[i]
            pltpu.make_async_copy(src.at[:, cols(h)], dst.at[:, cols(h)], out_sem.at[i]).start()

    def stage_c(h, c):
        lam = rate[h]
        into, out = column_weights(h)
        ti = lax.broadcasted_iota(jnp.int32, (TOK, TOK), 0)
        si = lax.broadcasted_iota(jnp.int32, (TOK, TOK), 1)
        dist = (ti - si).astype(F32)
        allowed = (ti >= si) & ((ti >= rho) == (si >= rho))
        mask = jnp.where(allowed, jnp.exp(-lam * jnp.maximum(dist, 0.0)), 0.0)
        qh, kh, vh = q_ref[:, cols(h)], k_ref[:, cols(h)], v_ref[:, cols(h)]
        weights = (dot(qh, kh, 1, 1) * scale * mask).astype(BF16)
        mixed = dot(weights, vh, 1, 0)
        wait_full(s_buf, 1, h)
        s_hi, s_lo = split(s_buf[h])
        mixed = mixed + into * (dot(qh, s_hi, 1, 0) + dot(qh, s_lo, 1, 0))
        centre = mixed - jnp.mean(mixed, axis=1, keepdims=True)
        r = lax.rsqrt(jnp.mean(centre * centre, axis=1, keepdims=True) + 1e-05)
        xhat = centre * r
        gain = gain_ref[cols(h)].reshape(1, HD)
        gate = g_ref[:, cols(h)].astype(F32)
        go = do_ref[:, cols(h)].astype(F32)
        sig = 1.0 / (1.0 + jnp.exp(-gate))
        silu = gate * sig
        ret_ref[:, cols(h)] = (silu * xhat * gain).astype(BF16)
        gox = go * xhat
        dgate_ref[:, cols(h)] = (gox * gain * (sig + silu * (1.0 - sig))).astype(BF16)
        gp[pl.ds(h, 1), :] = jnp.sum(gox * silu, axis=0, keepdims=True)
        dx = go * silu * gain
        dx = dx - jnp.mean(dx, axis=1, keepdims=True) - xhat * jnp.mean(
            dx * xhat, axis=1, keepdims=True
        )
        gm = dx * r
        e_hi, e_lo = split(gm * into)
        e_buf[h] = dot(qh, e_hi, 0, 0) + dot(qh, e_lo, 0, 0)
        to_owners(e_buf, r3, 2, h)
        low, rest = split(gm)
        gw = (dot(low, vh, 1, 1) * mask).astype(BF16)
        inter = dot(low, s_hi, 1, 1) + dot(low, s_lo, 1, 1) + dot(rest, s_hi, 1, 1)
        dq_ref[:, cols(h)] = (dot(gw, kh, 1, 0) * scale + inter * into).astype(BF16)
        dkp[h] = dot(gw, qh, 0, 0) * scale
        dvp[h] = dot(weights, low, 0, 0)
        store(h, 0, 1, 4)
        return c

    lax.fori_loop(0, heads, stage_c, 0)

    def gain_z(k, c):
        remote(gp, gz.at[z], gs.at[0], gr.at[0], context=ctx(x, z + k)).start()
        return c

    lax.fori_loop(1, ROW, gain_z, 0)
    gz[z] = gp[...]

    def backward_prompt(h, first, start):
        row = decay_row(h)

        def step(i, g):
            jz = ROW - 1 - i
            j = first + jz
            slot = lax.rem(z - jz + ROW, ROW)
            g = g + b_in[h, 0] * (pairs[0, 0] == j).astype(F32)
            g = g + b_in[h, 1] * (pairs[0, 1] == j).astype(F32)
            o4[h, slot] = g
            return r3[h, slot] + g * link(h, j, row)

        return lax.fori_loop(0, ROW, step, start)

    def stage_d(h, c):
        wait_row(r3, 2, h, False)

        @pl.when(jnp.logical_not(is_prompt))
        def _():
            row = decay_row(h)

            def side(sd, total):
                def step(i, g):
                    slot = lax.rem(z - sd * SPAN - (SPAN - 1 - i) + ROW, ROW)
                    o4[h, slot] = g
                    return r3[h, slot] + g * row

                return total + lax.fori_loop(0, SPAN, step, jnp.zeros((SL, HD), F32))

            b_out[h] = lax.fori_loop(0, ROW // SPAN, side, jnp.zeros((SL, HD), F32))
            pair = x // 3
            x_send(b_out.at[h], b_in.at[h, pair], 3, h, 2).start()
            x_send(b_out.at[h], b_in.at[h, pair], 3, h, 1).start()

        @pl.when(is_prompt)
        def _():
            x_send(c_out.at[h], b_in.at[h], 3, h, 0).wait_recv()

        @pl.when(x == 2)
        def _():
            t_out[h] = backward_prompt(h, ROW, jnp.zeros((SL, HD), F32))
            x_send(t_out.at[h], t_in.at[h], 2, h, 1).start()

        @pl.when(x == 1)
        def _():
            x_send(t_out.at[h], t_in.at[h], 2, h, 2).wait_recv()
            backward_prompt(h, 0, t_in[h])

        from_owner(o4, g_buf, 3, h)
        return c

    lax.fori_loop(0, heads, stage_d, 0)

    w = gz.at[pl.ds(0, ROW - 1)]
    remote(w, w, gs.at[0], gr.at[0], context=ctx(x, z + 1)).wait()

    gx_out[...] = lax.fori_loop(1, ROW, lambda i, a: a + gz[i], gz[0])

    def gain_x(k, c):
        remote(
            gx_out, gx.at[x], gs.at[1], gr.at[1], context=ctx(lax.rem(x + k, ROWS), z)
        ).start()
        return c

    lax.fori_loop(1, ROWS, gain_x, 0)
    gx[x] = gx_out[...]

    def gain_dp(k, c):
        remote(gd_out, gd.at[my_dp], gs.at[2], gr.at[2], dp=lax.rem(my_dp + k, n_dp)).start()
        return c

    def stage_e(h, c):
        wait_full(g_buf, 3, h)
        _, out = column_weights(h)
        out = out * scale
        g_hi, g_lo = split(g_buf[h])
        kh, vh = k_ref[:, cols(h)], v_ref[:, cols(h)]
        dk_ref[:, cols(h)] = (
            dkp[h] + out * (dot(vh, g_hi, 1, 1) + dot(vh, g_lo, 1, 1))
        ).astype(BF16)
        dv_ref[:, cols(h)] = (
            dvp[h] + out * (dot(kh, g_hi, 1, 0) + dot(kh, g_lo, 1, 0))
        ).astype(BF16)
        store(h, 2, 3)

        @pl.when(h == heads // 2)
        def _():
            w = gx.at[pl.ds(0, ROWS - 1)]
            remote(w, w, gs.at[1], gr.at[1], context=ctx(x, z + 1)).wait()
            gd_out[...] = gx[0] + gx[1] + gx[2] + gx[3]
            lax.fori_loop(1, n_dp, gain_dp, 0)
            gd[my_dp] = gd_out[...]

        return c

    lax.fori_loop(0, heads, stage_e, 0)

    w = gd.at[pl.ds(0, n_dp - 1)]
    remote(w, w, gs.at[2], gr.at[2], context=ctx(x, z + 1)).wait()
    token_total = TOK * ROW * ROWS * n_dp
    dgain_ref[...] = lax.fori_loop(1, n_dp, lambda i, a: a + gd[i], gd[0]) * (token_total**-0.5)

    def drain(h, c):
        wait_row(r1, 0, h, True)
        wait_row(o2, 1, h, True)
        wait_row(r3, 2, h, True)
        wait_row(o4, 3, h, True)

        @pl.when(x == 1)
        def _():
            x_send(t_out.at[h], t_in.at[h], 0, h, 2).wait_send()

        @pl.when(x == 2)
        def _():
            x_send(t_out.at[h], t_in.at[h], 2, h, 1).wait_send()

        @pl.when(is_prompt)
        def _():
            x_send(c_out.at[h], c_in.at[h], 1, h, 0).wait_send()

        @pl.when(jnp.logical_not(is_prompt))
        def _():
            x_send(c_out.at[h], b_in.at[h], 3, h, 1).wait_send()

        return c

    lax.fori_loop(0, heads, drain, 0)
    for i, (src, dst) in enumerate(results):
        pltpu.make_async_copy(src, dst, out_sem.at[i]).wait()


def finish_kernel(heads, *refs):
    given, out, held, sem_in, sem_out = refs[:6], refs[6:12], refs[12:17], refs[17], refs[18]
    loads = [pltpu.make_async_copy(given[i], held[i], sem_in.at[i]) for i in range(5)]
    stores = [pltpu.make_async_copy(held[i], out[i], sem_out.at[i]) for i in range(5)]
    for load in loads:
        load.start()
    for h in range(heads):
        out[5][pl.ds(h * HD, HD)] = given[5][pl.ds(h, 1), :].reshape(HD)
    for load, store in zip(loads, stores):
        load.wait()
        store.start()
    for store in stores:
        store.wait()


def solution(mesh):
    n_dp = mesh.shape["dp"]
    assert mesh.shape["context"] == ROW * ROWS

    def per_device(
        queries,
        key_rows,
        value_rows,
        gate_rows,
        out_grad,
        decay_rate,
        norm_gain,
        reset_offsets,
        pair_prompts,
    ):
        heads = decay_rate.shape[0]
        flat = jax.ShapeDtypeStruct(queries.shape, BF16)
        vmem = pl.BlockSpec(memory_space=pltpu.VMEM)
        smem = pl.BlockSpec(memory_space=pltpu.SMEM)
        state = pltpu.VMEM((heads, HD, HD), F32)
        slots = pltpu.VMEM((heads, ROW, SL, HD), F32)
        piece = pltpu.VMEM((heads, SL, HD), F32)
        two = pltpu.VMEM((heads, 2, SL, HD), F32)
        part = pltpu.VMEM((heads, TOK, HD), F32)
        small = pltpu.VMEM((8, HD), F32)
        dma = pltpu.SemaphoreType.DMA
        hbm = pl.BlockSpec(memory_space=pltpu.HBM)
        anywhere = pl.BlockSpec(memory_space=pl.ANY)
        held = pltpu.VMEM(queries.shape, BF16)
        outs = pl.pallas_call(
            functools.partial(kernel, heads, n_dp),
            out_shape=(flat, flat, flat, flat, flat, jax.ShapeDtypeStruct((8, HD), F32)),
            in_specs=[smem] * 3 + [hbm] * 6,
            out_specs=(hbm,) * 5 + (vmem,),
            scratch_shapes=[held] * 10
            + [
                pltpu.VMEM(norm_gain.shape, F32),
                state,
                slots,
                slots,
                state,
                state,
                slots,
                slots,
                state,
                piece,
                piece,
                two,
                two,
                piece,
                two,
                part,
                part,
                small,
                pltpu.VMEM((ROW, 8, HD), F32),
                small,
                pltpu.VMEM((ROWS, 8, HD), F32),
                small,
                pltpu.VMEM((n_dp, 8, HD), F32),
                dma((4, heads)),
                dma((4, heads)),
                dma((4, heads)),
                dma((4, heads)),
                dma((3,)),
                dma((3,)),
                dma((6,)),
                dma((5,)),
            ],
            compiler_params=pltpu.CompilerParams(
                collective_id=0, has_side_effects=True, vmem_limit_bytes=60 << 20
            ),
        )(
            decay_rate,
            reset_offsets,
            pair_prompts,
            queries,
            key_rows,
            value_rows,
            gate_rows,
            out_grad,
            norm_gain,
        )
        total = jax.ShapeDtypeStruct(norm_gain.shape, F32)
        return pl.pallas_call(
            functools.partial(finish_kernel, heads),
            out_shape=(flat,) * 5 + (total,),
            in_specs=[anywhere] * 5 + [vmem],
            out_specs=(hbm,) * 5 + (vmem,),
            scratch_shapes=[held] * 5 + [dma((5,)), dma((5,))],
            compiler_params=pltpu.CompilerParams(vmem_limit_bytes=60 << 20),
        )(*outs)

    rows = P(("dp", "context"), "tensor")
    in_specs = (rows,) * 5 + (P("tensor"), P("tensor"), P("dp", None), P("dp", None))
    return jax.shard_map(
        per_device,
        mesh=mesh,
        in_specs=in_specs,
        out_specs=(rows,) * 5 + (P("tensor"),),
        check_vma=False,
    )
```

```python
import functools

import jax
import jax.numpy as jnp
from jax import lax
from jax.experimental import pallas as pl
from jax.experimental.pallas import tpu as pltpu
from jax.sharding import PartitionSpec as P

MESH = pl.DeviceIdType.MESH
F32 = jnp.float32
BF16 = jnp.bfloat16

ROW = 8
ROWS = 4
HD = 256
TOK = 128
SL = HD // ROW
SPAN = 4
PARTS = 4
PR = HD // PARTS
LENT = (1, 0, 0, 0, 0)
LAG = (2, 3, 4, 5)
LAG_BACK = (6, 4, 2, 0)
LAG_SUM = 9
LAG_OWNED = 10


def dot(a, b, ca, cb):
    return lax.dot_general(a, b, (((ca,), (cb,)), ((), ())), preferred_element_type=F32)


def split(x):
    hi = x.astype(BF16)
    return hi, (x - hi.astype(F32)).astype(BF16)


def remote(src, dst, send_sem, recv_sem, **where):
    return pltpu.make_async_remote_copy(
        src_ref=src,
        dst_ref=dst,
        send_sem=send_sem,
        recv_sem=recv_sem,
        device_id=where,
        device_id_type=MESH,
    )


def pick(values, i):
    out = values[0]
    for n in range(1, len(values)):
        out = jnp.where(i == n, values[n], out)
    return out


def kernel(
    heads,
    n_dp,
    rate,
    resets,
    pairs,
    q_hbm,
    k_hbm,
    v_hbm,
    g_hbm,
    do_hbm,
    gain_hbm,
    ret_hbm,
    dq_hbm,
    dk_hbm,
    dv_hbm,
    dgate_hbm,
    dgain_ref,
    q_ref,
    k_ref,
    v_ref,
    g_ref,
    do_ref,
    ret_ref,
    dq_ref,
    dk_ref,
    dv_ref,
    dgate_ref,
    gain_ref,
    l_buf,
    s_buf,
    e_buf,
    g_buf,
    eo_buf,
    no_buf,
    r1,
    o2,
    r3,
    o4,
    t_out,
    t_in,
    seed,
    b_out,
    c_out,
    c_in,
    b_in,
    f_in,
    start,
    dkp,
    dvp,
    gp,
    gz,
    gx_out,
    gx,
    gd_out,
    gd,
    ss,
    rs,
    xs,
    xr,
    hs,
    hr,
    cs,
    cr,
    bs,
    br,
    gs,
    gr,
    in_sem,
    out_sem,
):
    me = lax.axis_index("context")
    my_dp = lax.axis_index("dp")
    x, z = me // ROW, lax.rem(me, ROW)
    m = lax.rem(z, SPAN)
    side = z // SPAN
    is_prompt = jnp.logical_and(x >= 1, x <= 2)
    is_response = jnp.logical_not(is_prompt)
    second = x >= 2
    mirror = x + 1 - 2 * lax.rem(x, 2)
    first = jnp.logical_and(is_response, m == 0)
    scale = HD**-0.5

    def ctx(xx, zz):
        return xx * ROW + lax.rem(zz + 2 * ROW, ROW)

    def lent(h):
        return pick(LENT, h) == 1

    def owns(h):
        return lent(h) == is_response

    def both(a, b):
        return jnp.logical_and(a, b)

    loads = [
        pltpu.make_async_copy(src, dst, in_sem.at[i])
        for i, (src, dst) in enumerate(
            (
                (k_hbm, k_ref),
                (v_hbm, v_ref),
                (q_hbm, q_ref),
                (g_hbm, g_ref),
                (do_hbm, do_ref),
                (gain_hbm, gain_ref),
            )
        )
    ]
    for load in loads:
        load.start()

    barrier = pltpu.get_barrier_semaphore()

    def greet(k, c):
        other = lax.rem(x + 2, ROWS) * ROW + z
        far = lax.rem(mirror + 2, ROWS) * ROW + z
        target = jnp.where(
            k < ROW,
            ctx(x, z + k),
            jnp.where(k < 2 * ROW, ctx(mirror, z + k), jnp.where(k == 2 * ROW, other, far)),
        )
        pl.semaphore_signal(barrier, inc=1, device_id={"context": target}, device_id_type=MESH)
        return c

    def greet_dp(k, c):
        pl.semaphore_signal(
            barrier, inc=1, device_id={"dp": lax.rem(my_dp + k, n_dp)}, device_id_type=MESH
        )
        return c

    lax.fori_loop(1, 2 * ROW + 2, greet, 0)
    lax.fori_loop(1, n_dp, greet_dp, 0)

    prompt_index = jnp.clip(me - ROW, 0, 2 * ROW - 1)
    rho = jnp.where(is_prompt, resets[0, prompt_index], TOK)

    def cols(h):
        return pl.ds(pl.multiple_of(h * HD, HD), HD)

    def column_weights(h):
        lam = rate[h]
        t = lax.broadcasted_iota(jnp.int32, (TOK, 1), 0)
        tf = t.astype(F32)
        into = jnp.where(t < rho, jnp.exp(-lam * (tf + 1.0)), 0.0)
        out = jnp.where(t >= lax.rem(rho, TOK), jnp.exp(-lam * (TOK - 1.0 - tf)), 0.0)
        return into, out

    def decay_row(h):
        return jnp.exp(jnp.full((1, HD), -float(TOK) * rate[h], F32))

    def link(h, j, row):
        return row * (resets[0, j] == TOK).astype(F32)

    def rows_of(zz):
        return pl.ds(pl.multiple_of(zz * SL, SL), SL)

    def part(p):
        return pl.ds(pl.multiple_of(p * PR, PR), PR)

    def spread(piece, target_row, landing, phase, h):
        def one(k, c):
            src, zz = piece(k)
            remote(
                src,
                landing(k),
                ss.at[phase, h],
                rs.at[phase, h],
                context=target_row * ROW + zz,
            ).start()
            return c

        lax.fori_loop(1, ROW, one, 0)

        @pl.when(target_row != x)
        def _():
            one(0, 0)

    def to_owners(src, dst, phase, h):
        def piece(k):
            zz = lax.rem(z + k, ROW)
            return src.at[h, rows_of(zz)], zz

        spread(piece, jnp.where(lent(h), mirror, x), lambda k: dst.at[h, k], phase, h)

        @pl.when(jnp.logical_not(lent(h)))
        def _():
            dst[h, 0] = src[h, rows_of(z)]

    def from_owner(src, dst, phase, h):
        def piece(k):
            return src.at[h, k], lax.rem(z - k + ROW, ROW)

        spread(piece, jnp.where(lent(h), mirror, x), lambda k: dst.at[h, rows_of(z)], phase, h)

        @pl.when(jnp.logical_not(lent(h)))
        def _():
            dst[h, rows_of(z)] = src[h, 0]

    def wait_slices(phase, h, sent):
        for n, when in ((ROW, lent(h)), (ROW - 1, jnp.logical_not(lent(h)))):

            @pl.when(when)
            def _():
                ref = r1.at[h, pl.ds(0, n)]
                c = remote(ref, ref, ss.at[phase, h], rs.at[phase, h], context=me)
                if sent:
                    c.wait_send()
                else:
                    c.wait_recv()

    def wait_bytes(count, send_sem, recv_sem, sent):
        ref = r1.at[0, pl.ds(0, count)]
        c = remote(ref, ref, send_sem, recv_sem, context=me)
        if sent:
            c.wait_send()
        else:
            c.wait_recv()

    def stage_a(h, c):
        _, out = column_weights(h)
        kw = k_ref[:, cols(h)].astype(F32) * (out * scale)
        hi, lo = split(kw)
        vh = v_ref[:, cols(h)]
        l_buf[h] = dot(hi, vh, 0, 0) + dot(lo, vh, 0, 0)
        return c

    loads[0].wait()
    loads[1].wait()
    lax.fori_loop(0, heads, stage_a, 0)
    pl.semaphore_wait(barrier, 2 * ROW + 1 + n_dp - 1)

    @pl.when(is_prompt)
    def _():
        def send_a(h, c):
            to_owners(l_buf, r1, 0, h)
            return c

        lax.fori_loop(0, heads, send_a, 0)

    def x_copy(src, dst, kind, h, xx):
        return remote(src, dst, xs.at[kind, h], xr.at[kind, h], context=xx * ROW + z)

    def hand_over(src, dst, kind, h, xx):
        @pl.when(xx != x)
        def _():
            x_copy(src, dst, kind, h, xx).start()

        @pl.when(xx == x)
        def _():
            dst[...] = src[...]

    def stage_b(h):
        wait_slices(0, h, False)

        @pl.when(second)
        def _():
            wait_bytes(1, xs.at[0, h], xr.at[0, h], False)
            start[...] = t_in[h]

        @pl.when(jnp.logical_not(second))
        def _():
            start[...] = jnp.zeros_like(start)

        row = decay_row(h)
        base = jnp.where(second, ROW, 0)

        def step(jz, carry):
            s, c0, c1 = carry
            j = base + jz
            slot = lax.rem(z - jz + ROW, ROW)
            o2[h, slot] = s
            s = s * link(h, j, row) + r1[h, slot]
            c0 = c0 + s * (pairs[0, 0] == j).astype(F32)
            c1 = c1 + s * (pairs[0, 1] == j).astype(F32)
            return s, c0, c1

        zero = jnp.zeros((SL, HD), F32)
        s, c0, c1 = lax.fori_loop(0, ROW, step, (start[...], zero, zero))
        c_out[h, 0] = c0
        c_out[h, 1] = c1

        @pl.when(jnp.logical_not(second))
        def _():
            t_out[h] = s
            x_copy(t_out.at[h], t_in.at[h], 0, h, jnp.where(lent(h), 3, 2)).start()

        half = second.astype(jnp.int32)
        hand_over(c_out.at[h, 0], c_in.at[h, half], 1, h, 0)
        hand_over(c_out.at[h, 1], c_in.at[h, half], 1, h, ROWS - 1)
        from_owner(o2, s_buf, 1, h)

    def wait_x(kind, h, sent):
        for n, when in ((1, lent(h)), (2, jnp.logical_not(lent(h)))):

            @pl.when(when)
            def _():
                wait_bytes(n, xs.at[kind, h], xr.at[kind, h], sent)

    def stage_seed(h):
        wait_x(1, h, False)
        seed[h] = c_in[h, 0] + c_in[h, 1]

        def one(sd, c):
            zz = sd * SPAN

            @pl.when(zz != z)
            def _():
                remote(
                    seed.at[h],
                    s_buf.at[h, rows_of(z)],
                    hs.at[0, h],
                    hr.at[0, h],
                    context=x * ROW + zz,
                ).start()

            @pl.when(zz == z)
            def _():
                s_buf[h, rows_of(z), :] = seed[h]

            return c

        lax.fori_loop(0, ROW // SPAN, one, 0)

    def chain(h):
        @pl.when(m == 0)
        def _():
            wait_bytes(ROW - 1, hs.at[0, h], hr.at[0, h], False)

        row = decay_row(h)

        def step(p, c):
            here = s_buf.at[h, part(p)]

            @pl.when(m > 0)
            def _():
                remote(here, here, cs.at[h, p], cr.at[h, p], context=me).wait_recv()

            @pl.when(m < SPAN - 1)
            def _():
                eo_buf[h, part(p), :] = s_buf[h, part(p), :] * row + l_buf[h, part(p), :]
                remote(
                    eo_buf.at[h, part(p)], here, cs.at[h, p], cr.at[h, p], context=me + 1
                ).start()

            return c

        lax.fori_loop(0, PARTS, step, 0)

    gp[...] = jnp.zeros_like(gp)
    for load in loads[2:]:
        load.wait()

    results = (
        (ret_ref, ret_hbm),
        (dq_ref, dq_hbm),
        (dk_ref, dk_hbm),
        (dv_ref, dv_hbm),
        (dgate_ref, dgate_hbm),
    )

    def store(h, *kinds):
        for i in kinds:
            src, dst = results[i]
            pltpu.make_async_copy(src.at[:, cols(h)], dst.at[:, cols(h)], out_sem.at[i]).start()

    def stage_c(h):
        lam = rate[h]
        into, out = column_weights(h)
        ti = lax.broadcasted_iota(jnp.int32, (TOK, TOK), 0)
        si = lax.broadcasted_iota(jnp.int32, (TOK, TOK), 1)
        dist = (ti - si).astype(F32)
        allowed = (ti >= si) & ((ti >= rho) == (si >= rho))
        mask = jnp.where(allowed, jnp.exp(-lam * jnp.maximum(dist, 0.0)), 0.0)
        qh, kh, vh = q_ref[:, cols(h)], k_ref[:, cols(h)], v_ref[:, cols(h)]
        weights = (dot(qh, kh, 1, 1) * scale * mask).astype(BF16)
        mixed = dot(weights, vh, 1, 0)
        s_hi, s_lo = split(s_buf[h])
        mixed = mixed + into * (dot(qh, s_hi, 1, 0) + dot(qh, s_lo, 1, 0))
        centre = mixed - jnp.mean(mixed, axis=1, keepdims=True)
        r = lax.rsqrt(jnp.mean(centre * centre, axis=1, keepdims=True) + 1e-05)
        xhat = centre * r
        gain = gain_ref[cols(h)].reshape(1, HD)
        gate = g_ref[:, cols(h)].astype(F32)
        go = do_ref[:, cols(h)].astype(F32)
        sig = 1.0 / (1.0 + jnp.exp(-gate))
        silu = gate * sig
        ret_ref[:, cols(h)] = (silu * xhat * gain).astype(BF16)
        gox = go * xhat
        dgate_ref[:, cols(h)] = (gox * gain * (sig + silu * (1.0 - sig))).astype(BF16)
        gp[pl.ds(h, 1), :] = jnp.sum(gox * silu, axis=0, keepdims=True)
        dx = go * silu * gain
        dx = dx - jnp.mean(dx, axis=1, keepdims=True) - xhat * jnp.mean(
            dx * xhat, axis=1, keepdims=True
        )
        gm = dx * r
        e_hi, e_lo = split(gm * into)
        e_buf[h] = dot(qh, e_hi, 0, 0) + dot(qh, e_lo, 0, 0)
        low, rest = split(gm)
        gw = (dot(low, vh, 1, 1) * mask).astype(BF16)
        inter = dot(low, s_hi, 1, 1) + dot(low, s_lo, 1, 1) + dot(rest, s_hi, 1, 1)
        dq_ref[:, cols(h)] = (dot(gw, kh, 1, 0) * scale + inter * into).astype(BF16)
        dkp[h] = dot(gw, qh, 0, 0) * scale
        dvp[h] = dot(weights, low, 0, 0)
        store(h, 0, 1, 4)

    def backward(h):
        @pl.when(m == SPAN - 1)
        def _():
            g_buf[h] = jnp.zeros((HD, HD), F32)

        row = decay_row(h)

        def step(p, c):
            here = g_buf.at[h, part(p)]

            @pl.when(m < SPAN - 1)
            def _():
                remote(here, here, bs.at[h, p], br.at[h, p], context=me).wait_recv()

            no_buf[h, part(p), :] = e_buf[h, part(p), :] + g_buf[h, part(p), :] * row

            @pl.when(m > 0)
            def _():
                remote(
                    no_buf.at[h, part(p)], here, bs.at[h, p], br.at[h, p], context=me - 1
                ).start()

            @pl.when(m == 0)
            def _():
                def one(k, cc):
                    zz = p * (ROW // PARTS) + k

                    @pl.when(zz != z)
                    def _():
                        remote(
                            no_buf.at[h, rows_of(zz)],
                            f_in.at[h, side],
                            hs.at[1, h],
                            hr.at[1, h],
                            context=x * ROW + zz,
                        ).start()

                    @pl.when(zz == z)
                    def _():
                        f_in[h, side] = no_buf[h, rows_of(zz), :]

                    return cc

                lax.fori_loop(0, ROW // PARTS, one, 0)

            return c

        lax.fori_loop(0, PARTS, step, 0)

    def stage_sum(h):
        @pl.when(m == 0)
        def _():
            wait_bytes(1, hs.at[1, h], hr.at[1, h], False)

        @pl.when(m > 0)
        def _():
            wait_bytes(2, hs.at[1, h], hr.at[1, h], False)

        b_out[h] = f_in[h, 0] + f_in[h, 1]
        pair = x // (ROWS - 1)
        for half in range(2):
            near = 2 - half
            target = jnp.where(lent(h), (1 - half) * (ROWS - 1), near)
            hand_over(b_out.at[h], b_in.at[h, pair], 3, h, target)

    def stage_d(h):
        wait_slices(2, h, False)
        wait_x(3, h, False)

        @pl.when(second)
        def _():
            start[...] = jnp.zeros_like(start)

        @pl.when(jnp.logical_not(second))
        def _():
            wait_bytes(1, xs.at[2, h], xr.at[2, h], False)
            start[...] = t_in[h]

        row = decay_row(h)
        base = jnp.where(second, ROW, 0)

        def step(i, g):
            jz = ROW - 1 - i
            j = base + jz
            slot = lax.rem(z - jz + ROW, ROW)
            g = g + b_in[h, 0] * (pairs[0, 0] == j).astype(F32)
            g = g + b_in[h, 1] * (pairs[0, 1] == j).astype(F32)
            o4[h, slot] = g
            return r3[h, slot] + g * link(h, j, row)

        g = lax.fori_loop(0, ROW, step, start[...])

        @pl.when(second)
        def _():
            t_out[h] = g
            x_copy(t_out.at[h], t_in.at[h], 2, h, jnp.where(lent(h), 0, 1)).start()

        from_owner(o4, g_buf, 3, h)

    def gain_row_send():
        def one(k, c):
            remote(gp, gz.at[z], gs.at[0], gr.at[0], context=ctx(x, z + k)).start()
            return c

        lax.fori_loop(1, ROW, one, 0)
        gz[z] = gp[...]

    def gain_x_send():
        ref = gz.at[pl.ds(0, ROW - 1)]
        remote(ref, ref, gs.at[0], gr.at[0], context=me).wait()
        gx_out[...] = lax.fori_loop(1, ROW, lambda i, a: a + gz[i], gz[0])

        def one(k, c):
            remote(
                gx_out, gx.at[x], gs.at[1], gr.at[1], context=lax.rem(x + k, ROWS) * ROW + z
            ).start()
            return c

        lax.fori_loop(1, ROWS, one, 0)
        gx[x] = gx_out[...]

    def gain_dp_send():
        ref = gx.at[pl.ds(0, ROWS - 1)]
        remote(ref, ref, gs.at[1], gr.at[1], context=me).wait()
        gd_out[...] = lax.fori_loop(1, ROWS, lambda i, a: a + gx[i], gx[0])

        def one(k, c):
            remote(
                gd_out, gd.at[my_dp], gs.at[2], gr.at[2], dp=lax.rem(my_dp + k, n_dp)
            ).start()
            return c

        lax.fori_loop(1, n_dp, one, 0)
        gd[my_dp] = gd_out[...]

    @pl.when(is_prompt)
    def _():
        def run_b(h, c):
            @pl.when(owns(h))
            def _():
                stage_b(h)

            return c

        lax.fori_loop(0, heads, run_b, 0)

    def valid(h):
        return both(h >= 0, h < heads)

    lag = jnp.where(is_prompt, 0, pick(LAG, m))
    lag_back = pick(LAG_BACK, m)

    def beat(i, c):
        @pl.when(is_response)
        def _():
            @pl.when(both(i < heads, owns(i)))
            def _():
                stage_b(i)

            @pl.when(valid(i - 1))
            def _():
                stage_seed(i - 1)

        hc = i - lag

        @pl.when(valid(hc))
        def _():
            @pl.when(is_prompt)
            def _():
                wait_slices(1, hc, False)

            @pl.when(is_response)
            def _():
                chain(hc)

            stage_c(hc)

            @pl.when(is_prompt)
            def _():
                to_owners(e_buf, r3, 2, hc)

        @pl.when(hc == heads)
        def _():
            gain_row_send()

        @pl.when(is_response)
        def _():
            hb = hc - lag_back

            @pl.when(valid(hb))
            def _():
                backward(hb)

            hg = i - LAG_SUM

            @pl.when(valid(hg))
            def _():
                stage_sum(hg)

        hd = i - LAG_OWNED

        @pl.when(both(valid(hd), owns(hd)))
        def _():
            stage_d(hd)

        return c

    lax.fori_loop(0, heads + LAG_OWNED, beat, 0)
    gain_x_send()

    def stage_e(h, c):
        @pl.when(is_prompt)
        def _():
            wait_slices(3, h, False)

        _, out = column_weights(h)
        out = out * scale
        g_hi, g_lo = split(g_buf[h])
        kh, vh = k_ref[:, cols(h)], v_ref[:, cols(h)]
        dk_ref[:, cols(h)] = (
            dkp[h] + out * (dot(vh, g_hi, 1, 1) + dot(vh, g_lo, 1, 1))
        ).astype(BF16)
        dv_ref[:, cols(h)] = (
            dvp[h] + out * (dot(kh, g_hi, 1, 0) + dot(kh, g_lo, 1, 0))
        ).astype(BF16)
        store(h, 2, 3)

        @pl.when(h == heads // 2)
        def _():
            gain_dp_send()

        return c

    lax.fori_loop(0, heads, stage_e, 0)

    w = gd.at[pl.ds(0, n_dp - 1)]
    remote(w, w, gs.at[2], gr.at[2], context=me).wait()
    token_total = TOK * ROW * ROWS * n_dp
    dgain_ref[...] = lax.fori_loop(1, n_dp, lambda i, a: a + gd[i], gd[0]) * (token_total**-0.5)

    def drain(h, c):
        @pl.when(is_prompt)
        def _():
            wait_slices(0, h, True)
            wait_slices(2, h, True)

        @pl.when(owns(h))
        def _():
            wait_slices(1, h, True)
            wait_slices(3, h, True)
            wait_x(1, h, True)

            @pl.when(second)
            def _():
                wait_bytes(1, xs.at[2, h], xr.at[2, h], True)

            @pl.when(jnp.logical_not(second))
            def _():
                wait_bytes(1, xs.at[0, h], xr.at[0, h], True)

        @pl.when(is_response)
        def _():
            wait_x(3, h, True)

            @pl.when(m == 0)
            def _():
                wait_bytes(1, hs.at[0, h], hr.at[0, h], True)
                wait_bytes(ROW - 1, hs.at[1, h], hr.at[1, h], True)

            @pl.when(m > 0)
            def _():
                wait_bytes(2, hs.at[0, h], hr.at[0, h], True)

            def step(p, cc):
                ref = no_buf.at[h, part(p)]

                @pl.when(m < SPAN - 1)
                def _():
                    remote(ref, ref, cs.at[h, p], cr.at[h, p], context=me).wait_send()

                @pl.when(m > 0)
                def _():
                    remote(ref, ref, bs.at[h, p], br.at[h, p], context=me).wait_send()

                return cc

            lax.fori_loop(0, PARTS, step, 0)

        return c

    lax.fori_loop(0, heads, drain, 0)
    for i, (src, dst) in enumerate(results):
        pltpu.make_async_copy(src, dst, out_sem.at[i]).wait()


def finish_kernel(heads, *refs):
    given, out, held, sem_in, sem_out = refs[:6], refs[6:12], refs[12:17], refs[17], refs[18]
    loads = [pltpu.make_async_copy(given[i], held[i], sem_in.at[i]) for i in range(5)]
    stores = [pltpu.make_async_copy(held[i], out[i], sem_out.at[i]) for i in range(5)]
    for load in loads:
        load.start()
    for h in range(heads):
        out[5][pl.ds(h * HD, HD)] = given[5][pl.ds(h, 1), :].reshape(HD)
    for load, store in zip(loads, stores):
        load.wait()
        store.start()
    for store in stores:
        store.wait()


def solution(mesh):
    n_dp = mesh.shape["dp"]
    assert mesh.shape["context"] == ROW * ROWS

    def per_device(
        queries,
        key_rows,
        value_rows,
        gate_rows,
        out_grad,
        decay_rate,
        norm_gain,
        reset_offsets,
        pair_prompts,
    ):
        heads = decay_rate.shape[0]
        flat = jax.ShapeDtypeStruct(queries.shape, BF16)
        vmem = pl.BlockSpec(memory_space=pltpu.VMEM)
        smem = pl.BlockSpec(memory_space=pltpu.SMEM)
        state = pltpu.VMEM((heads, HD, HD), F32)
        slots = pltpu.VMEM((heads, ROW, SL, HD), F32)
        piece = pltpu.VMEM((heads, SL, HD), F32)
        two = pltpu.VMEM((heads, 2, SL, HD), F32)
        part = pltpu.VMEM((heads, TOK, HD), F32)
        small = pltpu.VMEM((8, HD), F32)
        dma = pltpu.SemaphoreType.DMA
        hbm = pl.BlockSpec(memory_space=pltpu.HBM)
        anywhere = pl.BlockSpec(memory_space=pl.ANY)
        held = pltpu.VMEM(queries.shape, BF16)
        outs = pl.pallas_call(
            functools.partial(kernel, heads, n_dp),
            out_shape=(flat, flat, flat, flat, flat, jax.ShapeDtypeStruct((8, HD), F32)),
            in_specs=[smem] * 3 + [hbm] * 6,
            out_specs=(hbm,) * 5 + (vmem,),
            scratch_shapes=[held] * 10
            + [
                pltpu.VMEM(norm_gain.shape, F32),
            ]
            + [state] * 6
            + [slots] * 4
            + [piece] * 4
            + [two] * 4
            + [
                pltpu.VMEM((SL, HD), F32),
                part,
                part,
                small,
                pltpu.VMEM((ROW, 8, HD), F32),
                small,
                pltpu.VMEM((ROWS, 8, HD), F32),
                small,
                pltpu.VMEM((n_dp, 8, HD), F32),
                dma((4, heads)),
                dma((4, heads)),
                dma((4, heads)),
                dma((4, heads)),
                dma((2, heads)),
                dma((2, heads)),
                dma((heads, PARTS)),
                dma((heads, PARTS)),
                dma((heads, PARTS)),
                dma((heads, PARTS)),
                dma((3,)),
                dma((3,)),
                dma((6,)),
                dma((5,)),
            ],
            compiler_params=pltpu.CompilerParams(
                collective_id=0, has_side_effects=True, vmem_limit_bytes=60 << 20
            ),
        )(
            decay_rate,
            reset_offsets,
            pair_prompts,
            queries,
            key_rows,
            value_rows,
            gate_rows,
            out_grad,
            norm_gain,
        )
        total = jax.ShapeDtypeStruct(norm_gain.shape, F32)
        return pl.pallas_call(
            functools.partial(finish_kernel, heads),
            out_shape=(flat,) * 5 + (total,),
            in_specs=[anywhere] * 5 + [vmem],
            out_specs=(hbm,) * 5 + (vmem,),
            scratch_shapes=[held] * 5 + [dma((5,)), dma((5,))],
            compiler_params=pltpu.CompilerParams(vmem_limit_bytes=60 << 20),
        )(*outs)

    rows = P(("dp", "context"), "tensor")
    in_specs = (rows,) * 5 + (P("tensor"), P("tensor"), P("dp", None), P("dp", None))
    return jax.shard_map(
        per_device,
        mesh=mesh,
        in_specs=in_specs,
        out_specs=(rows,) * 5 + (P("tensor"),),
        check_vma=False,
    )
```

```python
import functools

import jax
import jax.numpy as jnp
from jax import lax
from jax.experimental import pallas as pl
from jax.experimental.pallas import tpu as pltpu
from jax.sharding import PartitionSpec as P

MESH = pl.DeviceIdType.MESH
F32 = jnp.float32
BF16 = jnp.bfloat16

ROW = 8
ROWS = 4
HD = 256
TOK = 128
SL = HD // ROW
SPAN = 4
PARTS = 4
PR = HD // PARTS
LENT = (1, 0, 0, 0, 0)
LAG = (2, 3, 4, 5)
LAG_BACK = (6, 4, 2, 0)
LAG_SUM = 9
LAG_OWNED = 10
LAG_LENT = 13
TURN = 1


def dot(a, b, ca, cb):
    return lax.dot_general(a, b, (((ca,), (cb,)), ((), ())), preferred_element_type=F32)


def split(x):
    hi = x.astype(BF16)
    return hi, (x - hi.astype(F32)).astype(BF16)


def remote(src, dst, send_sem, recv_sem, **where):
    return pltpu.make_async_remote_copy(
        src_ref=src,
        dst_ref=dst,
        send_sem=send_sem,
        recv_sem=recv_sem,
        device_id=where,
        device_id_type=MESH,
    )


def pick(values, i):
    out = values[0]
    for n in range(1, len(values)):
        out = jnp.where(i == n, values[n], out)
    return out


def kernel(
    heads,
    n_dp,
    rate,
    resets,
    pairs,
    q_hbm,
    k_hbm,
    v_hbm,
    g_hbm,
    do_hbm,
    gain_hbm,
    ret_hbm,
    dq_hbm,
    dk_hbm,
    dv_hbm,
    dgate_hbm,
    dgain_ref,
    q_ref,
    k_ref,
    v_ref,
    g_ref,
    do_ref,
    ret_ref,
    dq_ref,
    dk_ref,
    dv_ref,
    dgate_ref,
    gain_ref,
    l_buf,
    s_buf,
    e_buf,
    g_buf,
    eo_buf,
    no_buf,
    r1,
    o2,
    r3,
    o4,
    t_out,
    t_in,
    seed,
    b_out,
    c_out,
    c_in,
    b_in,
    f_in,
    start,
    dkp,
    dvp,
    gp,
    gz,
    gx_out,
    gx,
    gd_out,
    gd,
    ss,
    rs,
    xs,
    xr,
    hs,
    hr,
    cs,
    cr,
    bs,
    br,
    gs,
    gr,
    in_sem,
    out_sem,
):
    me = lax.axis_index("context")
    my_dp = lax.axis_index("dp")
    x, z = me // ROW, lax.rem(me, ROW)
    m = lax.rem(z, SPAN)
    side = z // SPAN
    is_prompt = jnp.logical_and(x >= 1, x <= 2)
    is_response = jnp.logical_not(is_prompt)
    second = x >= 2
    mirror = x + 1 - 2 * lax.rem(x, 2)
    first = jnp.logical_and(is_response, m == 0)
    scale = HD**-0.5

    def ctx(xx, zz):
        return xx * ROW + lax.rem(zz + 2 * ROW, ROW)

    def lent(h):
        return pick(LENT, h) == 1

    def owns(h):
        return lent(h) == is_response

    def both(a, b):
        return jnp.logical_and(a, b)

    loads = [
        pltpu.make_async_copy(src, dst, in_sem.at[i])
        for i, (src, dst) in enumerate(
            (
                (k_hbm, k_ref),
                (v_hbm, v_ref),
                (q_hbm, q_ref),
                (g_hbm, g_ref),
                (do_hbm, do_ref),
                (gain_hbm, gain_ref),
            )
        )
    ]
    for load in loads:
        load.start()

    barrier = pltpu.get_barrier_semaphore()

    def greet(k, c):
        other = lax.rem(x + 2, ROWS) * ROW + z
        far = lax.rem(mirror + 2, ROWS) * ROW + z
        target = jnp.where(
            k < ROW,
            ctx(x, z + k),
            jnp.where(k < 2 * ROW, ctx(mirror, z + k), jnp.where(k == 2 * ROW, other, far)),
        )
        pl.semaphore_signal(barrier, inc=1, device_id={"context": target}, device_id_type=MESH)
        return c

    def greet_dp(k, c):
        pl.semaphore_signal(
            barrier, inc=1, device_id={"dp": lax.rem(my_dp + k, n_dp)}, device_id_type=MESH
        )
        return c

    lax.fori_loop(1, 2 * ROW + 2, greet, 0)
    lax.fori_loop(1, n_dp, greet_dp, 0)

    prompt_index = jnp.clip(me - ROW, 0, 2 * ROW - 1)
    rho = jnp.where(is_prompt, resets[0, prompt_index], TOK)

    def cols(h):
        return pl.ds(pl.multiple_of(h * HD, HD), HD)

    def column_weights(h):
        lam = rate[h]
        t = lax.broadcasted_iota(jnp.int32, (TOK, 1), 0)
        tf = t.astype(F32)
        into = jnp.where(t < rho, jnp.exp(-lam * (tf + 1.0)), 0.0)
        out = jnp.where(t >= lax.rem(rho, TOK), jnp.exp(-lam * (TOK - 1.0 - tf)), 0.0)
        return into, out

    def decay_row(h):
        return jnp.exp(jnp.full((1, HD), -float(TOK) * rate[h], F32))

    def link(h, j, row):
        return row * (resets[0, j] == TOK).astype(F32)

    def rows_of(zz):
        return pl.ds(pl.multiple_of(zz * SL, SL), SL)

    def part(p):
        return pl.ds(pl.multiple_of(p * PR, PR), PR)

    def spread(piece, target_row, landing, phase, h):
        def one(k, c):
            src, zz = piece(k)
            remote(
                src,
                landing(k),
                ss.at[phase, h],
                rs.at[phase, h],
                context=target_row * ROW + zz,
            ).start()
            return c

        lax.fori_loop(1, ROW, one, 0)

        @pl.when(target_row != x)
        def _():
            one(0, 0)

    def to_owners(src, dst, phase, h):
        def piece(k):
            zz = lax.rem(z + k, ROW)
            return src.at[h, rows_of(zz)], zz

        spread(piece, jnp.where(lent(h), mirror, x), lambda k: dst.at[h, k], phase, h)

        @pl.when(jnp.logical_not(lent(h)))
        def _():
            dst[h, 0] = src[h, rows_of(z)]

    def from_owner(src, dst, phase, h):
        def piece(k):
            return src.at[h, k], lax.rem(z - k + ROW, ROW)

        spread(piece, jnp.where(lent(h), mirror, x), lambda k: dst.at[h, rows_of(z)], phase, h)

        @pl.when(jnp.logical_not(lent(h)))
        def _():
            dst[h, rows_of(z)] = src[h, 0]

    def wait_slices(phase, h, sent):
        for n, when in ((ROW, lent(h)), (ROW - 1, jnp.logical_not(lent(h)))):

            @pl.when(when)
            def _():
                ref = r1.at[h, pl.ds(0, n)]
                c = remote(ref, ref, ss.at[phase, h], rs.at[phase, h], context=me)
                if sent:
                    c.wait_send()
                else:
                    c.wait_recv()

    def wait_bytes(count, send_sem, recv_sem, sent):
        ref = r1.at[0, pl.ds(0, count)]
        c = remote(ref, ref, send_sem, recv_sem, context=me)
        if sent:
            c.wait_send()
        else:
            c.wait_recv()

    def stage_a(h, c):
        _, out = column_weights(h)
        kw = k_ref[:, cols(h)].astype(F32) * (out * scale)
        hi, lo = split(kw)
        vh = v_ref[:, cols(h)]
        l_buf[h] = dot(hi, vh, 0, 0) + dot(lo, vh, 0, 0)
        return c

    loads[0].wait()
    loads[1].wait()
    lax.fori_loop(0, heads, stage_a, 0)
    pl.semaphore_wait(barrier, 2 * ROW + 1 + n_dp - 1)

    @pl.when(is_prompt)
    def _():
        def send_a(h, c):
            to_owners(l_buf, r1, 0, h)
            return c

        lax.fori_loop(0, heads, send_a, 0)

    def x_copy(src, dst, kind, h, xx):
        return remote(src, dst, xs.at[kind, h], xr.at[kind, h], context=xx * ROW + z)

    def hand_over(src, dst, kind, h, xx):
        @pl.when(xx != x)
        def _():
            x_copy(src, dst, kind, h, xx).start()

        @pl.when(xx == x)
        def _():
            dst[...] = src[...]

    def stage_b(h):
        wait_slices(0, h, False)

        @pl.when(second)
        def _():
            wait_bytes(1, xs.at[0, h], xr.at[0, h], False)
            start[...] = t_in[h]

        @pl.when(jnp.logical_not(second))
        def _():
            start[...] = jnp.zeros_like(start)

        row = decay_row(h)
        base = jnp.where(second, ROW, 0)

        def step(jz, carry):
            s, c0, c1 = carry
            j = base + jz
            slot = lax.rem(z - jz + ROW, ROW)
            o2[h, slot] = s
            s = s * link(h, j, row) + r1[h, slot]
            c0 = c0 + s * (pairs[0, 0] == j).astype(F32)
            c1 = c1 + s * (pairs[0, 1] == j).astype(F32)
            return s, c0, c1

        zero = jnp.zeros((SL, HD), F32)
        s, c0, c1 = lax.fori_loop(0, ROW, step, (start[...], zero, zero))
        c_out[h, 0] = c0
        c_out[h, 1] = c1

        @pl.when(jnp.logical_not(second))
        def _():
            t_out[h] = s
            x_copy(t_out.at[h], t_in.at[h], 0, h, jnp.where(lent(h), 3, 2)).start()

        half = second.astype(jnp.int32)
        hand_over(c_out.at[h, 0], c_in.at[h, half], 1, h, 0)
        hand_over(c_out.at[h, 1], c_in.at[h, half], 1, h, ROWS - 1)
        from_owner(o2, s_buf, 1, h)

    def wait_x(kind, h, sent):
        for n, when in ((1, lent(h)), (2, jnp.logical_not(lent(h)))):

            @pl.when(when)
            def _():
                wait_bytes(n, xs.at[kind, h], xr.at[kind, h], sent)

    def stage_seed(h):
        wait_x(1, h, False)
        seed[h] = c_in[h, 0] + c_in[h, 1]

        def one(sd, c):
            zz = sd * SPAN

            @pl.when(zz != z)
            def _():
                remote(
                    seed.at[h],
                    s_buf.at[h, rows_of(z)],
                    hs.at[0, h],
                    hr.at[0, h],
                    context=x * ROW + zz,
                ).start()

            @pl.when(zz == z)
            def _():
                s_buf[h, rows_of(z), :] = seed[h]

            return c

        lax.fori_loop(0, ROW // SPAN, one, 0)

    def chain(h):
        @pl.when(m == 0)
        def _():
            wait_bytes(ROW - 1, hs.at[0, h], hr.at[0, h], False)

        row = decay_row(h)

        def step(p, c):
            here = s_buf.at[h, part(p)]

            @pl.when(m > 0)
            def _():
                remote(here, here, cs.at[h, p], cr.at[h, p], context=me).wait_recv()

            @pl.when(m < SPAN - 1)
            def _():
                eo_buf[h, part(p), :] = s_buf[h, part(p), :] * row + l_buf[h, part(p), :]
                remote(
                    eo_buf.at[h, part(p)], here, cs.at[h, p], cr.at[h, p], context=me + 1
                ).start()

            return c

        lax.fori_loop(0, PARTS, step, 0)

    gp[...] = jnp.zeros_like(gp)
    for load in loads[2:]:
        load.wait()

    results = (
        (ret_ref, ret_hbm),
        (dq_ref, dq_hbm),
        (dk_ref, dk_hbm),
        (dv_ref, dv_hbm),
        (dgate_ref, dgate_hbm),
    )

    def store(h, *kinds):
        for i in kinds:
            src, dst = results[i]
            pltpu.make_async_copy(src.at[:, cols(h)], dst.at[:, cols(h)], out_sem.at[i]).start()

    def stage_c(h):
        lam = rate[h]
        into, out = column_weights(h)
        ti = lax.broadcasted_iota(jnp.int32, (TOK, TOK), 0)
        si = lax.broadcasted_iota(jnp.int32, (TOK, TOK), 1)
        dist = (ti - si).astype(F32)
        allowed = (ti >= si) & ((ti >= rho) == (si >= rho))
        mask = jnp.where(allowed, jnp.exp(-lam * jnp.maximum(dist, 0.0)), 0.0)
        qh, kh, vh = q_ref[:, cols(h)], k_ref[:, cols(h)], v_ref[:, cols(h)]
        weights = (dot(qh, kh, 1, 1) * scale * mask).astype(BF16)
        mixed = dot(weights, vh, 1, 0)
        s_hi, s_lo = split(s_buf[h])
        mixed = mixed + into * (dot(qh, s_hi, 1, 0) + dot(qh, s_lo, 1, 0))
        centre = mixed - jnp.mean(mixed, axis=1, keepdims=True)
        r = lax.rsqrt(jnp.mean(centre * centre, axis=1, keepdims=True) + 1e-05)
        xhat = centre * r
        gain = gain_ref[cols(h)].reshape(1, HD)
        gate = g_ref[:, cols(h)].astype(F32)
        go = do_ref[:, cols(h)].astype(F32)
        sig = 1.0 / (1.0 + jnp.exp(-gate))
        silu = gate * sig
        ret_ref[:, cols(h)] = (silu * xhat * gain).astype(BF16)
        gox = go * xhat
        dgate_ref[:, cols(h)] = (gox * gain * (sig + silu * (1.0 - sig))).astype(BF16)
        gp[pl.ds(h, 1), :] = jnp.sum(gox * silu, axis=0, keepdims=True)
        dx = go * silu * gain
        dx = dx - jnp.mean(dx, axis=1, keepdims=True) - xhat * jnp.mean(
            dx * xhat, axis=1, keepdims=True
        )
        gm = dx * r
        e_hi, e_lo = split(gm * into)
        e_buf[h] = dot(qh, e_hi, 0, 0) + dot(qh, e_lo, 0, 0)
        low, rest = split(gm)
        gw = (dot(low, vh, 1, 1) * mask).astype(BF16)
        inter = dot(low, s_hi, 1, 1) + dot(low, s_lo, 1, 1) + dot(rest, s_hi, 1, 1)
        dq_ref[:, cols(h)] = (dot(gw, kh, 1, 0) * scale + inter * into).astype(BF16)
        dkp[h] = dot(gw, qh, 0, 0) * scale
        dvp[h] = dot(weights, low, 0, 0)
        store(h, 0, 1, 4)

    def backward(h):
        @pl.when(m == SPAN - 1)
        def _():
            g_buf[h] = jnp.zeros((HD, HD), F32)

        row = decay_row(h)

        def step(p, c):
            here = g_buf.at[h, part(p)]

            @pl.when(m < SPAN - 1)
            def _():
                remote(here, here, bs.at[h, p], br.at[h, p], context=me).wait_recv()

            no_buf[h, part(p), :] = e_buf[h, part(p), :] + g_buf[h, part(p), :] * row

            @pl.when(m > 0)
            def _():
                remote(
                    no_buf.at[h, part(p)], here, bs.at[h, p], br.at[h, p], context=me - 1
                ).start()

            @pl.when(m == 0)
            def _():
                def one(k, cc):
                    zz = p * (ROW // PARTS) + k

                    @pl.when(zz != z)
                    def _():
                        remote(
                            no_buf.at[h, rows_of(zz)],
                            f_in.at[h, side],
                            hs.at[1, h],
                            hr.at[1, h],
                            context=x * ROW + zz,
                        ).start()

                    @pl.when(zz == z)
                    def _():
                        f_in[h, side] = no_buf[h, rows_of(zz), :]

                    return cc

                lax.fori_loop(0, ROW // PARTS, one, 0)

            return c

        lax.fori_loop(0, PARTS, step, 0)

    def stage_sum(h):
        @pl.when(m == 0)
        def _():
            wait_bytes(1, hs.at[1, h], hr.at[1, h], False)

        @pl.when(m > 0)
        def _():
            wait_bytes(2, hs.at[1, h], hr.at[1, h], False)

        b_out[h] = f_in[h, 0] + f_in[h, 1]
        pair = x // (ROWS - 1)
        for half in range(2):
            near = 2 - half
            target = jnp.where(lent(h), (1 - half) * (ROWS - 1), near)
            hand_over(b_out.at[h], b_in.at[h, pair], 3, h, target)

    def stage_d(h):
        wait_slices(2, h, False)
        wait_x(3, h, False)

        @pl.when(second)
        def _():
            start[...] = jnp.zeros_like(start)

        @pl.when(jnp.logical_not(second))
        def _():
            wait_bytes(1, xs.at[2, h], xr.at[2, h], False)
            start[...] = t_in[h]

        row = decay_row(h)
        base = jnp.where(second, ROW, 0)

        def step(i, g):
            jz = ROW - 1 - i
            j = base + jz
            slot = lax.rem(z - jz + ROW, ROW)
            g = g + b_in[h, 0] * (pairs[0, 0] == j).astype(F32)
            g = g + b_in[h, 1] * (pairs[0, 1] == j).astype(F32)
            o4[h, slot] = g
            return r3[h, slot] + g * link(h, j, row)

        g = lax.fori_loop(0, ROW, step, start[...])

        @pl.when(second)
        def _():
            t_out[h] = g
            x_copy(t_out.at[h], t_in.at[h], 2, h, jnp.where(lent(h), 0, 1)).start()

        from_owner(o4, g_buf, 3, h)

    def gain_row_send():
        def one(k, c):
            remote(gp, gz.at[z], gs.at[0], gr.at[0], context=ctx(x, z + k)).start()
            return c

        lax.fori_loop(1, ROW, one, 0)
        gz[z] = gp[...]

    def gain_x_send():
        ref = gz.at[pl.ds(0, ROW - 1)]
        remote(ref, ref, gs.at[0], gr.at[0], context=me).wait()
        gx_out[...] = lax.fori_loop(1, ROW, lambda i, a: a + gz[i], gz[0])

        def one(k, c):
            remote(
                gx_out, gx.at[x], gs.at[1], gr.at[1], context=lax.rem(x + k, ROWS) * ROW + z
            ).start()
            return c

        lax.fori_loop(1, ROWS, one, 0)
        gx[x] = gx_out[...]

    def gain_dp_send():
        ref = gx.at[pl.ds(0, ROWS - 1)]
        remote(ref, ref, gs.at[1], gr.at[1], context=me).wait()
        gd_out[...] = lax.fori_loop(1, ROWS, lambda i, a: a + gx[i], gx[0])

        def one(k, c):
            remote(
                gd_out, gd.at[my_dp], gs.at[2], gr.at[2], dp=lax.rem(my_dp + k, n_dp)
            ).start()
            return c

        lax.fori_loop(1, n_dp, one, 0)
        gd[my_dp] = gd_out[...]

    @pl.when(is_prompt)
    def _():
        def run_b(h, c):
            @pl.when(owns(h))
            def _():
                stage_b(h)

            return c

        lax.fori_loop(0, heads, run_b, 0)

    def valid(h):
        return both(h >= 0, h < heads)

    lag = jnp.where(is_prompt, 0, pick(LAG, m))
    lag_back = pick(LAG_BACK, m)

    def beat(i, c):
        @pl.when(is_response)
        def _():
            @pl.when(both(i < heads, owns(i)))
            def _():
                stage_b(i)

            @pl.when(valid(i - 1))
            def _():
                stage_seed(i - 1)

        hc = i - lag

        @pl.when(valid(hc))
        def _():
            @pl.when(is_prompt)
            def _():
                wait_slices(1, hc, False)

            @pl.when(is_response)
            def _():
                chain(hc)

            stage_c(hc)

            @pl.when(is_prompt)
            def _():
                to_owners(e_buf, r3, 2, hc)

        @pl.when(hc == heads)
        def _():
            gain_row_send()

        @pl.when(is_response)
        def _():
            hb = hc - lag_back

            @pl.when(valid(hb))
            def _():
                backward(hb)

            hg = i - LAG_SUM

            @pl.when(valid(hg))
            def _():
                stage_sum(hg)

        hd = i - jnp.where(is_response, LAG_LENT, LAG_OWNED)

        @pl.when(both(valid(hd), owns(hd)))
        def _():
            stage_d(hd)

        return c

    lax.fori_loop(0, heads + max(LAG_OWNED, LAG_LENT), beat, 0)
    gain_x_send()

    def stage_e(i, c):
        h = jnp.where(is_prompt, lax.rem(i + TURN, heads), i)
        @pl.when(is_prompt)
        def _():
            wait_slices(3, h, False)

        _, out = column_weights(h)
        out = out * scale
        g_hi, g_lo = split(g_buf[h])
        kh, vh = k_ref[:, cols(h)], v_ref[:, cols(h)]
        dk_ref[:, cols(h)] = (
            dkp[h] + out * (dot(vh, g_hi, 1, 1) + dot(vh, g_lo, 1, 1))
        ).astype(BF16)
        dv_ref[:, cols(h)] = (
            dvp[h] + out * (dot(kh, g_hi, 1, 0) + dot(kh, g_lo, 1, 0))
        ).astype(BF16)
        store(h, 2, 3)

        @pl.when(i == heads // 2)
        def _():
            gain_dp_send()

        return c

    lax.fori_loop(0, heads, stage_e, 0)

    w = gd.at[pl.ds(0, n_dp - 1)]
    remote(w, w, gs.at[2], gr.at[2], context=me).wait()
    token_total = TOK * ROW * ROWS * n_dp
    dgain_ref[...] = lax.fori_loop(1, n_dp, lambda i, a: a + gd[i], gd[0]) * (token_total**-0.5)

    def drain(h, c):
        @pl.when(is_prompt)
        def _():
            wait_slices(0, h, True)
            wait_slices(2, h, True)

        @pl.when(owns(h))
        def _():
            wait_slices(1, h, True)
            wait_slices(3, h, True)
            wait_x(1, h, True)

            @pl.when(second)
            def _():
                wait_bytes(1, xs.at[2, h], xr.at[2, h], True)

            @pl.when(jnp.logical_not(second))
            def _():
                wait_bytes(1, xs.at[0, h], xr.at[0, h], True)

        @pl.when(is_response)
        def _():
            wait_x(3, h, True)

            @pl.when(m == 0)
            def _():
                wait_bytes(1, hs.at[0, h], hr.at[0, h], True)
                wait_bytes(ROW - 1, hs.at[1, h], hr.at[1, h], True)

            @pl.when(m > 0)
            def _():
                wait_bytes(2, hs.at[0, h], hr.at[0, h], True)

            def step(p, cc):
                ref = no_buf.at[h, part(p)]

                @pl.when(m < SPAN - 1)
                def _():
                    remote(ref, ref, cs.at[h, p], cr.at[h, p], context=me).wait_send()

                @pl.when(m > 0)
                def _():
                    remote(ref, ref, bs.at[h, p], br.at[h, p], context=me).wait_send()

                return cc

            lax.fori_loop(0, PARTS, step, 0)

        return c

    lax.fori_loop(0, heads, drain, 0)
    for i, (src, dst) in enumerate(results):
        pltpu.make_async_copy(src, dst, out_sem.at[i]).wait()


def finish_kernel(heads, *refs):
    given, out, held, sem_in, sem_out = refs[:6], refs[6:12], refs[12:17], refs[17], refs[18]
    loads = [pltpu.make_async_copy(given[i], held[i], sem_in.at[i]) for i in range(5)]
    stores = [pltpu.make_async_copy(held[i], out[i], sem_out.at[i]) for i in range(5)]
    for load in loads:
        load.start()
    for h in range(heads):
        out[5][pl.ds(h * HD, HD)] = given[5][pl.ds(h, 1), :].reshape(HD)
    for load, store in zip(loads, stores):
        load.wait()
        store.start()
    for store in stores:
        store.wait()


def solution(mesh):
    n_dp = mesh.shape["dp"]
    assert mesh.shape["context"] == ROW * ROWS

    def per_device(
        queries,
        key_rows,
        value_rows,
        gate_rows,
        out_grad,
        decay_rate,
        norm_gain,
        reset_offsets,
        pair_prompts,
    ):
        heads = decay_rate.shape[0]
        flat = jax.ShapeDtypeStruct(queries.shape, BF16)
        vmem = pl.BlockSpec(memory_space=pltpu.VMEM)
        smem = pl.BlockSpec(memory_space=pltpu.SMEM)
        state = pltpu.VMEM((heads, HD, HD), F32)
        slots = pltpu.VMEM((heads, ROW, SL, HD), F32)
        piece = pltpu.VMEM((heads, SL, HD), F32)
        two = pltpu.VMEM((heads, 2, SL, HD), F32)
        part = pltpu.VMEM((heads, TOK, HD), F32)
        small = pltpu.VMEM((8, HD), F32)
        dma = pltpu.SemaphoreType.DMA
        hbm = pl.BlockSpec(memory_space=pltpu.HBM)
        anywhere = pl.BlockSpec(memory_space=pl.ANY)
        held = pltpu.VMEM(queries.shape, BF16)
        outs = pl.pallas_call(
            functools.partial(kernel, heads, n_dp),
            out_shape=(flat, flat, flat, flat, flat, jax.ShapeDtypeStruct((8, HD), F32)),
            in_specs=[smem] * 3 + [hbm] * 6,
            out_specs=(hbm,) * 5 + (vmem,),
            scratch_shapes=[held] * 10
            + [
                pltpu.VMEM(norm_gain.shape, F32),
            ]
            + [state] * 6
            + [slots] * 4
            + [piece] * 4
            + [two] * 4
            + [
                pltpu.VMEM((SL, HD), F32),
                part,
                part,
                small,
                pltpu.VMEM((ROW, 8, HD), F32),
                small,
                pltpu.VMEM((ROWS, 8, HD), F32),
                small,
                pltpu.VMEM((n_dp, 8, HD), F32),
                dma((4, heads)),
                dma((4, heads)),
                dma((4, heads)),
                dma((4, heads)),
                dma((2, heads)),
                dma((2, heads)),
                dma((heads, PARTS)),
                dma((heads, PARTS)),
                dma((heads, PARTS)),
                dma((heads, PARTS)),
                dma((3,)),
                dma((3,)),
                dma((6,)),
                dma((5,)),
            ],
            compiler_params=pltpu.CompilerParams(
                collective_id=0, has_side_effects=True, vmem_limit_bytes=60 << 20
            ),
        )(
            decay_rate,
            reset_offsets,
            pair_prompts,
            queries,
            key_rows,
            value_rows,
            gate_rows,
            out_grad,
            norm_gain,
        )
        total = jax.ShapeDtypeStruct(norm_gain.shape, F32)
        return pl.pallas_call(
            functools.partial(finish_kernel, heads),
            out_shape=(flat,) * 5 + (total,),
            in_specs=[anywhere] * 5 + [vmem],
            out_specs=(hbm,) * 5 + (vmem,),
            scratch_shapes=[held] * 5 + [dma((5,)), dma((5,))],
            compiler_params=pltpu.CompilerParams(vmem_limit_bytes=60 << 20),
        )(*outs)

    rows = P(("dp", "context"), "tensor")
    in_specs = (rows,) * 5 + (P("tensor"), P("tensor"), P("dp", None), P("dp", None))
    return jax.shard_map(
        per_device,
        mesh=mesh,
        in_specs=in_specs,
        out_specs=(rows,) * 5 + (P("tensor"),),
        check_vma=False,
    )
```

```python
import functools

import jax
import jax.numpy as jnp
from jax import lax
from jax.experimental import pallas as pl
from jax.experimental.pallas import tpu as pltpu
from jax.sharding import PartitionSpec as P

MESH = pl.DeviceIdType.MESH
F32 = jnp.float32
BF16 = jnp.bfloat16

ROW = 8
ROWS = 4
HD = 256
TOK = 128
SL = HD // ROW
SPAN = 4
PARTS = 4
PR = HD // PARTS
LENT = (1, 0, 0, 0, 0)
LAG = (2, 3, 4, 5)
LAG_BACK = (6, 4, 2, 0)
LAG_SUM = 9
LAG_OWNED = 10
LAG_LENT = 13
TURN = 1


def dot(a, b, ca, cb):
    return lax.dot_general(a, b, (((ca,), (cb,)), ((), ())), preferred_element_type=F32)


def split(x):
    hi = x.astype(BF16)
    return hi, (x - hi.astype(F32)).astype(BF16)


def remote(src, dst, send_sem, recv_sem, **where):
    return pltpu.make_async_remote_copy(
        src_ref=src,
        dst_ref=dst,
        send_sem=send_sem,
        recv_sem=recv_sem,
        device_id=where,
        device_id_type=MESH,
    )


def pick(values, i):
    out = values[0]
    for n in range(1, len(values)):
        out = jnp.where(i == n, values[n], out)
    return out


def kernel(
    heads,
    n_dp,
    rate_hbm,
    resets_hbm,
    pairs_hbm,
    q_hbm,
    k_hbm,
    v_hbm,
    g_hbm,
    do_hbm,
    gain_hbm,
    ret_hbm,
    dq_hbm,
    dk_hbm,
    dv_hbm,
    dgate_hbm,
    dgain_hbm,
    q_ref,
    k_ref,
    v_ref,
    g_ref,
    do_ref,
    ret_ref,
    dq_ref,
    dk_ref,
    dv_ref,
    dgate_ref,
    gain_ref,
    rate,
    resets,
    pairs,
    dgain_ref,
    l_buf,
    s_buf,
    e_buf,
    g_buf,
    eo_buf,
    no_buf,
    r1,
    o2,
    r3,
    o4,
    t_out,
    t_in,
    seed,
    b_out,
    c_out,
    c_in,
    b_in,
    f_in,
    start,
    dkp,
    dvp,
    gp,
    gz,
    gx_out,
    gx,
    gd_out,
    gd,
    ss,
    rs,
    xs,
    xr,
    hs,
    hr,
    cs,
    cr,
    bs,
    br,
    gs,
    gr,
    in_sem,
    out_sem,
):
    me = lax.axis_index("context")
    my_dp = lax.axis_index("dp")
    x, z = me // ROW, lax.rem(me, ROW)
    m = lax.rem(z, SPAN)
    side = z // SPAN
    is_prompt = jnp.logical_and(x >= 1, x <= 2)
    is_response = jnp.logical_not(is_prompt)
    second = x >= 2
    mirror = x + 1 - 2 * lax.rem(x, 2)
    first = jnp.logical_and(is_response, m == 0)
    scale = HD**-0.5

    def ctx(xx, zz):
        return xx * ROW + lax.rem(zz + 2 * ROW, ROW)

    def lent(h):
        return pick(LENT, h) == 1

    def owns(h):
        return lent(h) == is_response

    def both(a, b):
        return jnp.logical_and(a, b)

    loads = [
        pltpu.make_async_copy(src, dst, in_sem.at[i])
        for i, (src, dst) in enumerate(
            (
                (rate_hbm, rate),
                (resets_hbm, resets),
                (pairs_hbm, pairs),
                (k_hbm, k_ref),
                (v_hbm, v_ref),
                (q_hbm, q_ref),
                (g_hbm, g_ref),
                (do_hbm, do_ref),
                (gain_hbm, gain_ref),
            )
        )
    ]
    for load in loads:
        load.start()

    barrier = pltpu.get_barrier_semaphore()

    def greet(k, c):
        other = lax.rem(x + 2, ROWS) * ROW + z
        far = lax.rem(mirror + 2, ROWS) * ROW + z
        target = jnp.where(
            k < ROW,
            ctx(x, z + k),
            jnp.where(k < 2 * ROW, ctx(mirror, z + k), jnp.where(k == 2 * ROW, other, far)),
        )
        pl.semaphore_signal(barrier, inc=1, device_id={"context": target}, device_id_type=MESH)
        return c

    def greet_dp(k, c):
        pl.semaphore_signal(
            barrier, inc=1, device_id={"dp": lax.rem(my_dp + k, n_dp)}, device_id_type=MESH
        )
        return c

    lax.fori_loop(1, 2 * ROW + 2, greet, 0)
    lax.fori_loop(1, n_dp, greet_dp, 0)

    for load in loads[:3]:
        load.wait()

    prompt_index = jnp.clip(me - ROW, 0, 2 * ROW - 1)
    rho = jnp.where(is_prompt, resets[0, prompt_index], TOK)

    def cols(h):
        return pl.ds(pl.multiple_of(h * HD, HD), HD)

    def column_weights(h):
        lam = rate[h]
        t = lax.broadcasted_iota(jnp.int32, (TOK, 1), 0)
        tf = t.astype(F32)
        into = jnp.where(t < rho, jnp.exp(-lam * (tf + 1.0)), 0.0)
        out = jnp.where(t >= lax.rem(rho, TOK), jnp.exp(-lam * (TOK - 1.0 - tf)), 0.0)
        return into, out

    def decay_row(h):
        return jnp.exp(jnp.full((1, HD), -float(TOK) * rate[h], F32))

    def link(h, j, row):
        return row * (resets[0, j] == TOK).astype(F32)

    def rows_of(zz):
        return pl.ds(pl.multiple_of(zz * SL, SL), SL)

    def part(p):
        return pl.ds(pl.multiple_of(p * PR, PR), PR)

    def spread(piece, target_row, landing, phase, h):
        def one(k, c):
            src, zz = piece(k)
            remote(
                src,
                landing(k),
                ss.at[phase, h],
                rs.at[phase, h],
                context=target_row * ROW + zz,
            ).start()
            return c

        lax.fori_loop(1, ROW, one, 0)

        @pl.when(target_row != x)
        def _():
            one(0, 0)

    def to_owners(src, dst, phase, h):
        def piece(k):
            zz = lax.rem(z + k, ROW)
            return src.at[h, rows_of(zz)], zz

        spread(piece, jnp.where(lent(h), mirror, x), lambda k: dst.at[h, k], phase, h)

        @pl.when(jnp.logical_not(lent(h)))
        def _():
            dst[h, 0] = src[h, rows_of(z)]

    def from_owner(src, dst, phase, h):
        def piece(k):
            return src.at[h, k], lax.rem(z - k + ROW, ROW)

        spread(piece, jnp.where(lent(h), mirror, x), lambda k: dst.at[h, rows_of(z)], phase, h)

        @pl.when(jnp.logical_not(lent(h)))
        def _():
            dst[h, rows_of(z)] = src[h, 0]

    def wait_slices(phase, h, sent):
        for n, when in ((ROW, lent(h)), (ROW - 1, jnp.logical_not(lent(h)))):

            @pl.when(when)
            def _():
                ref = r1.at[h, pl.ds(0, n)]
                c = remote(ref, ref, ss.at[phase, h], rs.at[phase, h], context=me)
                if sent:
                    c.wait_send()
                else:
                    c.wait_recv()

    def wait_bytes(count, send_sem, recv_sem, sent):
        ref = r1.at[0, pl.ds(0, count)]
        c = remote(ref, ref, send_sem, recv_sem, context=me)
        if sent:
            c.wait_send()
        else:
            c.wait_recv()

    def stage_a(h, c):
        _, out = column_weights(h)
        kw = k_ref[:, cols(h)].astype(F32) * (out * scale)
        hi, lo = split(kw)
        vh = v_ref[:, cols(h)]
        l_buf[h] = dot(hi, vh, 0, 0) + dot(lo, vh, 0, 0)
        return c

    loads[3].wait()
    loads[4].wait()
    lax.fori_loop(0, heads, stage_a, 0)
    pl.semaphore_wait(barrier, 2 * ROW + 1 + n_dp - 1)

    @pl.when(is_prompt)
    def _():
        def send_a(h, c):
            to_owners(l_buf, r1, 0, h)
            return c

        lax.fori_loop(0, heads, send_a, 0)

    def x_copy(src, dst, kind, h, xx):
        return remote(src, dst, xs.at[kind, h], xr.at[kind, h], context=xx * ROW + z)

    def hand_over(src, dst, kind, h, xx):
        @pl.when(xx != x)
        def _():
            x_copy(src, dst, kind, h, xx).start()

        @pl.when(xx == x)
        def _():
            dst[...] = src[...]

    def stage_b(h):
        wait_slices(0, h, False)

        @pl.when(second)
        def _():
            wait_bytes(1, xs.at[0, h], xr.at[0, h], False)
            start[...] = t_in[h]

        @pl.when(jnp.logical_not(second))
        def _():
            start[...] = jnp.zeros_like(start)

        row = decay_row(h)
        base = jnp.where(second, ROW, 0)

        def step(jz, carry):
            s, c0, c1 = carry
            j = base + jz
            slot = lax.rem(z - jz + ROW, ROW)
            o2[h, slot] = s
            s = s * link(h, j, row) + r1[h, slot]
            c0 = c0 + s * (pairs[0, 0] == j).astype(F32)
            c1 = c1 + s * (pairs[0, 1] == j).astype(F32)
            return s, c0, c1

        zero = jnp.zeros((SL, HD), F32)
        s, c0, c1 = lax.fori_loop(0, ROW, step, (start[...], zero, zero))
        c_out[h, 0] = c0
        c_out[h, 1] = c1

        @pl.when(jnp.logical_not(second))
        def _():
            t_out[h] = s
            x_copy(t_out.at[h], t_in.at[h], 0, h, jnp.where(lent(h), 3, 2)).start()

        half = second.astype(jnp.int32)
        hand_over(c_out.at[h, 0], c_in.at[h, half], 1, h, 0)
        hand_over(c_out.at[h, 1], c_in.at[h, half], 1, h, ROWS - 1)
        from_owner(o2, s_buf, 1, h)

    def wait_x(kind, h, sent):
        for n, when in ((1, lent(h)), (2, jnp.logical_not(lent(h)))):

            @pl.when(when)
            def _():
                wait_bytes(n, xs.at[kind, h], xr.at[kind, h], sent)

    def stage_seed(h):
        wait_x(1, h, False)
        seed[h] = c_in[h, 0] + c_in[h, 1]

        def one(sd, c):
            zz = sd * SPAN

            @pl.when(zz != z)
            def _():
                remote(
                    seed.at[h],
                    s_buf.at[h, rows_of(z)],
                    hs.at[0, h],
                    hr.at[0, h],
                    context=x * ROW + zz,
                ).start()

            @pl.when(zz == z)
            def _():
                s_buf[h, rows_of(z), :] = seed[h]

            return c

        lax.fori_loop(0, ROW // SPAN, one, 0)

    def chain(h):
        @pl.when(m == 0)
        def _():
            wait_bytes(ROW - 1, hs.at[0, h], hr.at[0, h], False)

        row = decay_row(h)

        def step(p, c):
            here = s_buf.at[h, part(p)]

            @pl.when(m > 0)
            def _():
                remote(here, here, cs.at[h, p], cr.at[h, p], context=me).wait_recv()

            @pl.when(m < SPAN - 1)
            def _():
                eo_buf[h, part(p), :] = s_buf[h, part(p), :] * row + l_buf[h, part(p), :]
                remote(
                    eo_buf.at[h, part(p)], here, cs.at[h, p], cr.at[h, p], context=me + 1
                ).start()

            return c

        lax.fori_loop(0, PARTS, step, 0)

    gp[...] = jnp.zeros_like(gp)
    for load in loads[5:]:
        load.wait()

    results = (
        (ret_ref, ret_hbm),
        (dq_ref, dq_hbm),
        (dk_ref, dk_hbm),
        (dv_ref, dv_hbm),
        (dgate_ref, dgate_hbm),
    )

    def store(h, *kinds):
        for i in kinds:
            src, dst = results[i]
            pltpu.make_async_copy(src.at[:, cols(h)], dst.at[:, cols(h)], out_sem.at[i]).start()

    def stage_c(h):
        lam = rate[h]
        into, out = column_weights(h)
        ti = lax.broadcasted_iota(jnp.int32, (TOK, TOK), 0)
        si = lax.broadcasted_iota(jnp.int32, (TOK, TOK), 1)
        dist = (ti - si).astype(F32)
        allowed = (ti >= si) & ((ti >= rho) == (si >= rho))
        mask = jnp.where(allowed, jnp.exp(-lam * jnp.maximum(dist, 0.0)), 0.0)
        qh, kh, vh = q_ref[:, cols(h)], k_ref[:, cols(h)], v_ref[:, cols(h)]
        weights = (dot(qh, kh, 1, 1) * scale * mask).astype(BF16)
        mixed = dot(weights, vh, 1, 0)
        s_hi, s_lo = split(s_buf[h])
        mixed = mixed + into * (dot(qh, s_hi, 1, 0) + dot(qh, s_lo, 1, 0))
        centre = mixed - jnp.mean(mixed, axis=1, keepdims=True)
        r = lax.rsqrt(jnp.mean(centre * centre, axis=1, keepdims=True) + 1e-05)
        xhat = centre * r
        gain = gain_ref[cols(h)].reshape(1, HD)
        gate = g_ref[:, cols(h)].astype(F32)
        go = do_ref[:, cols(h)].astype(F32)
        sig = 1.0 / (1.0 + jnp.exp(-gate))
        silu = gate * sig
        ret_ref[:, cols(h)] = (silu * xhat * gain).astype(BF16)
        gox = go * xhat
        dgate_ref[:, cols(h)] = (gox * gain * (sig + silu * (1.0 - sig))).astype(BF16)
        gp[pl.ds(h, 1), :] = jnp.sum(gox * silu, axis=0, keepdims=True)
        dx = go * silu * gain
        dx = dx - jnp.mean(dx, axis=1, keepdims=True) - xhat * jnp.mean(
            dx * xhat, axis=1, keepdims=True
        )
        gm = dx * r
        e_hi, e_lo = split(gm * into)
        e_buf[h] = dot(qh, e_hi, 0, 0) + dot(qh, e_lo, 0, 0)
        low, rest = split(gm)
        gw = (dot(low, vh, 1, 1) * mask).astype(BF16)
        inter = dot(low, s_hi, 1, 1) + dot(low, s_lo, 1, 1) + dot(rest, s_hi, 1, 1)
        dq_ref[:, cols(h)] = (dot(gw, kh, 1, 0) * scale + inter * into).astype(BF16)
        dkp[h] = dot(gw, qh, 0, 0) * scale
        dvp[h] = dot(weights, low, 0, 0)
        store(h, 0, 1, 4)

    def backward(h):
        @pl.when(m == SPAN - 1)
        def _():
            g_buf[h] = jnp.zeros((HD, HD), F32)

        row = decay_row(h)

        def step(p, c):
            here = g_buf.at[h, part(p)]

            @pl.when(m < SPAN - 1)
            def _():
                remote(here, here, bs.at[h, p], br.at[h, p], context=me).wait_recv()

            no_buf[h, part(p), :] = e_buf[h, part(p), :] + g_buf[h, part(p), :] * row

            @pl.when(m > 0)
            def _():
                remote(
                    no_buf.at[h, part(p)], here, bs.at[h, p], br.at[h, p], context=me - 1
                ).start()

            @pl.when(m == 0)
            def _():
                def one(k, cc):
                    zz = p * (ROW // PARTS) + k

                    @pl.when(zz != z)
                    def _():
                        remote(
                            no_buf.at[h, rows_of(zz)],
                            f_in.at[h, side],
                            hs.at[1, h],
                            hr.at[1, h],
                            context=x * ROW + zz,
                        ).start()

                    @pl.when(zz == z)
                    def _():
                        f_in[h, side] = no_buf[h, rows_of(zz), :]

                    return cc

                lax.fori_loop(0, ROW // PARTS, one, 0)

            return c

        lax.fori_loop(0, PARTS, step, 0)

    def stage_sum(h):
        @pl.when(m == 0)
        def _():
            wait_bytes(1, hs.at[1, h], hr.at[1, h], False)

        @pl.when(m > 0)
        def _():
            wait_bytes(2, hs.at[1, h], hr.at[1, h], False)

        b_out[h] = f_in[h, 0] + f_in[h, 1]
        pair = x // (ROWS - 1)
        for half in range(2):
            near = 2 - half
            target = jnp.where(lent(h), (1 - half) * (ROWS - 1), near)
            hand_over(b_out.at[h], b_in.at[h, pair], 3, h, target)

    def stage_d(h):
        wait_slices(2, h, False)
        wait_x(3, h, False)

        @pl.when(second)
        def _():
            start[...] = jnp.zeros_like(start)

        @pl.when(jnp.logical_not(second))
        def _():
            wait_bytes(1, xs.at[2, h], xr.at[2, h], False)
            start[...] = t_in[h]

        row = decay_row(h)
        base = jnp.where(second, ROW, 0)

        def step(i, g):
            jz = ROW - 1 - i
            j = base + jz
            slot = lax.rem(z - jz + ROW, ROW)
            g = g + b_in[h, 0] * (pairs[0, 0] == j).astype(F32)
            g = g + b_in[h, 1] * (pairs[0, 1] == j).astype(F32)
            o4[h, slot] = g
            return r3[h, slot] + g * link(h, j, row)

        g = lax.fori_loop(0, ROW, step, start[...])

        @pl.when(second)
        def _():
            t_out[h] = g
            x_copy(t_out.at[h], t_in.at[h], 2, h, jnp.where(lent(h), 0, 1)).start()

        from_owner(o4, g_buf, 3, h)

    def gain_row_send():
        def one(k, c):
            remote(gp, gz.at[z], gs.at[0], gr.at[0], context=ctx(x, z + k)).start()
            return c

        lax.fori_loop(1, ROW, one, 0)
        gz[z] = gp[...]

    def gain_x_send():
        ref = gz.at[pl.ds(0, ROW - 1)]
        remote(ref, ref, gs.at[0], gr.at[0], context=me).wait()
        gx_out[...] = lax.fori_loop(1, ROW, lambda i, a: a + gz[i], gz[0])

        def one(k, c):
            remote(
                gx_out, gx.at[x], gs.at[1], gr.at[1], context=lax.rem(x + k, ROWS) * ROW + z
            ).start()
            return c

        lax.fori_loop(1, ROWS, one, 0)
        gx[x] = gx_out[...]

    def gain_dp_send():
        ref = gx.at[pl.ds(0, ROWS - 1)]
        remote(ref, ref, gs.at[1], gr.at[1], context=me).wait()
        gd_out[...] = lax.fori_loop(1, ROWS, lambda i, a: a + gx[i], gx[0])

        def one(k, c):
            remote(
                gd_out, gd.at[my_dp], gs.at[2], gr.at[2], dp=lax.rem(my_dp + k, n_dp)
            ).start()
            return c

        lax.fori_loop(1, n_dp, one, 0)
        gd[my_dp] = gd_out[...]

    @pl.when(is_prompt)
    def _():
        def run_b(h, c):
            @pl.when(owns(h))
            def _():
                stage_b(h)

            return c

        lax.fori_loop(0, heads, run_b, 0)

    def valid(h):
        return both(h >= 0, h < heads)

    lag = jnp.where(is_prompt, 0, pick(LAG, m))
    lag_back = pick(LAG_BACK, m)

    def beat(i, c):
        @pl.when(is_response)
        def _():
            @pl.when(both(i < heads, owns(i)))
            def _():
                stage_b(i)

            @pl.when(valid(i - 1))
            def _():
                stage_seed(i - 1)

        hc = i - lag

        @pl.when(valid(hc))
        def _():
            @pl.when(is_prompt)
            def _():
                wait_slices(1, hc, False)

            @pl.when(is_response)
            def _():
                chain(hc)

            stage_c(hc)

            @pl.when(is_prompt)
            def _():
                to_owners(e_buf, r3, 2, hc)

        @pl.when(hc == heads)
        def _():
            gain_row_send()

        @pl.when(is_response)
        def _():
            hb = hc - lag_back

            @pl.when(valid(hb))
            def _():
                backward(hb)

            hg = i - LAG_SUM

            @pl.when(valid(hg))
            def _():
                stage_sum(hg)

        hd = i - jnp.where(is_response, LAG_LENT, LAG_OWNED)

        @pl.when(both(valid(hd), owns(hd)))
        def _():
            stage_d(hd)

        return c

    lax.fori_loop(0, heads + max(LAG_OWNED, LAG_LENT), beat, 0)
    gain_x_send()

    def stage_e(i, c):
        h = jnp.where(is_prompt, lax.rem(i + TURN, heads), i)
        @pl.when(is_prompt)
        def _():
            wait_slices(3, h, False)

        _, out = column_weights(h)
        out = out * scale
        g_hi, g_lo = split(g_buf[h])
        kh, vh = k_ref[:, cols(h)], v_ref[:, cols(h)]
        dk_ref[:, cols(h)] = (
            dkp[h] + out * (dot(vh, g_hi, 1, 1) + dot(vh, g_lo, 1, 1))
        ).astype(BF16)
        dv_ref[:, cols(h)] = (
            dvp[h] + out * (dot(kh, g_hi, 1, 0) + dot(kh, g_lo, 1, 0))
        ).astype(BF16)
        store(h, 2, 3)

        @pl.when(i == heads // 2)
        def _():
            gain_dp_send()

        return c

    lax.fori_loop(0, heads, stage_e, 0)

    w = gd.at[pl.ds(0, n_dp - 1)]
    remote(w, w, gs.at[2], gr.at[2], context=me).wait()
    token_total = TOK * ROW * ROWS * n_dp
    dgain_ref[...] = lax.fori_loop(1, n_dp, lambda i, a: a + gd[i], gd[0]) * (token_total**-0.5)
    last = pltpu.make_async_copy(dgain_ref, dgain_hbm, out_sem.at[5])
    last.start()

    def drain(h, c):
        @pl.when(is_prompt)
        def _():
            wait_slices(0, h, True)
            wait_slices(2, h, True)

        @pl.when(owns(h))
        def _():
            wait_slices(1, h, True)
            wait_slices(3, h, True)
            wait_x(1, h, True)

            @pl.when(second)
            def _():
                wait_bytes(1, xs.at[2, h], xr.at[2, h], True)

            @pl.when(jnp.logical_not(second))
            def _():
                wait_bytes(1, xs.at[0, h], xr.at[0, h], True)

        @pl.when(is_response)
        def _():
            wait_x(3, h, True)

            @pl.when(m == 0)
            def _():
                wait_bytes(1, hs.at[0, h], hr.at[0, h], True)
                wait_bytes(ROW - 1, hs.at[1, h], hr.at[1, h], True)

            @pl.when(m > 0)
            def _():
                wait_bytes(2, hs.at[0, h], hr.at[0, h], True)

            def step(p, cc):
                ref = no_buf.at[h, part(p)]

                @pl.when(m < SPAN - 1)
                def _():
                    remote(ref, ref, cs.at[h, p], cr.at[h, p], context=me).wait_send()

                @pl.when(m > 0)
                def _():
                    remote(ref, ref, bs.at[h, p], br.at[h, p], context=me).wait_send()

                return cc

            lax.fori_loop(0, PARTS, step, 0)

        return c

    lax.fori_loop(0, heads, drain, 0)
    for i, (src, dst) in enumerate(results):
        pltpu.make_async_copy(src, dst, out_sem.at[i]).wait()
    last.wait()


def finish_kernel(heads, *refs):
    given, out, held, total, sem_in, sem_out = (
        refs[:6],
        refs[6:12],
        refs[12:18],
        refs[18],
        refs[19],
        refs[20],
    )
    loads = [pltpu.make_async_copy(given[i], held[i], sem_in.at[i]) for i in range(6)]
    stores = [pltpu.make_async_copy(held[i], out[i], sem_out.at[i]) for i in range(5)]
    stores.append(pltpu.make_async_copy(total, out[5], sem_out.at[5]))
    for load in loads:
        load.start()
    for load, store in zip(loads[:5], stores):
        load.wait()
        store.start()
    loads[5].wait()
    for h in range(heads):
        total[pl.ds(h * HD, HD)] = held[5][pl.ds(h, 1), :].reshape(HD)
    stores[5].start()
    for store in stores:
        store.wait()


def solution(mesh):
    n_dp = mesh.shape["dp"]
    assert mesh.shape["context"] == ROW * ROWS

    def per_device(
        queries,
        key_rows,
        value_rows,
        gate_rows,
        out_grad,
        decay_rate,
        norm_gain,
        reset_offsets,
        pair_prompts,
    ):
        heads = decay_rate.shape[0]
        flat = jax.ShapeDtypeStruct(queries.shape, BF16)
        state = pltpu.VMEM((heads, HD, HD), F32)
        slots = pltpu.VMEM((heads, ROW, SL, HD), F32)
        piece = pltpu.VMEM((heads, SL, HD), F32)
        two = pltpu.VMEM((heads, 2, SL, HD), F32)
        part = pltpu.VMEM((heads, TOK, HD), F32)
        small = pltpu.VMEM((8, HD), F32)
        dma = pltpu.SemaphoreType.DMA
        hbm = pl.BlockSpec(memory_space=pltpu.HBM)
        anywhere = pl.BlockSpec(memory_space=pl.ANY)
        held = pltpu.VMEM(queries.shape, BF16)
        outs = pl.pallas_call(
            functools.partial(kernel, heads, n_dp),
            out_shape=(flat, flat, flat, flat, flat, jax.ShapeDtypeStruct((8, HD), F32)),
            in_specs=[hbm] * 9,
            out_specs=(hbm,) * 6,
            scratch_shapes=[held] * 10
            + [
                pltpu.VMEM(norm_gain.shape, F32),
                pltpu.SMEM(decay_rate.shape, F32),
                pltpu.SMEM(reset_offsets.shape, jnp.int32),
                pltpu.SMEM(pair_prompts.shape, jnp.int32),
                small,
            ]
            + [state] * 6
            + [slots] * 4
            + [piece] * 4
            + [two] * 4
            + [
                pltpu.VMEM((SL, HD), F32),
                part,
                part,
                small,
                pltpu.VMEM((ROW, 8, HD), F32),
                small,
                pltpu.VMEM((ROWS, 8, HD), F32),
                small,
                pltpu.VMEM((n_dp, 8, HD), F32),
                dma((4, heads)),
                dma((4, heads)),
                dma((4, heads)),
                dma((4, heads)),
                dma((2, heads)),
                dma((2, heads)),
                dma((heads, PARTS)),
                dma((heads, PARTS)),
                dma((heads, PARTS)),
                dma((heads, PARTS)),
                dma((3,)),
                dma((3,)),
                dma((9,)),
                dma((6,)),
            ],
            compiler_params=pltpu.CompilerParams(
                collective_id=0, has_side_effects=True, vmem_limit_bytes=60 << 20
            ),
        )(
            decay_rate,
            reset_offsets,
            pair_prompts,
            queries,
            key_rows,
            value_rows,
            gate_rows,
            out_grad,
            norm_gain,
        )
        total = jax.ShapeDtypeStruct(norm_gain.shape, F32)
        return pl.pallas_call(
            functools.partial(finish_kernel, heads),
            out_shape=(flat,) * 5 + (total,),
            in_specs=[anywhere] * 6,
            out_specs=(hbm,) * 6,
            scratch_shapes=[held] * 5
            + [small, pltpu.VMEM(norm_gain.shape, F32), dma((6,)), dma((6,))],
            compiler_params=pltpu.CompilerParams(vmem_limit_bytes=60 << 20),
        )(*outs)

    rows = P(("dp", "context"), "tensor")
    in_specs = (rows,) * 5 + (P("tensor"), P("tensor"), P("dp", None), P("dp", None))
    return jax.shard_map(
        per_device,
        mesh=mesh,
        in_specs=in_specs,
        out_specs=(rows,) * 5 + (P("tensor"),),
        check_vma=False,
    )
```

```python
import functools

import jax
import jax.numpy as jnp
from jax import lax
from jax.experimental import pallas as pl
from jax.experimental.pallas import tpu as pltpu
from jax.sharding import PartitionSpec as P

MESH = pl.DeviceIdType.MESH
F32 = jnp.float32
BF16 = jnp.bfloat16

ROW = 8
ROWS = 4
HD = 256
TOK = 128
SL = HD // ROW
SPAN = 4
PARTS = 4
PR = HD // PARTS
LENT = (1, 0, 0, 0, 0)
LAG = (2, 3, 4, 5)
LAG_BACK = (6, 4, 2, 0)
LAG_SUM = 9
LAG_OWNED = 10
LAG_LENT = 13
TURN = 1


def dot(a, b, ca, cb):
    return lax.dot_general(a, b, (((ca,), (cb,)), ((), ())), preferred_element_type=F32)


def split(x):
    hi = x.astype(BF16)
    return hi, (x - hi.astype(F32)).astype(BF16)


def remote(src, dst, send_sem, recv_sem, **where):
    return pltpu.make_async_remote_copy(
        src_ref=src,
        dst_ref=dst,
        send_sem=send_sem,
        recv_sem=recv_sem,
        device_id=where,
        device_id_type=MESH,
    )


def pick(values, i):
    out = values[0]
    for n in range(1, len(values)):
        out = jnp.where(i == n, values[n], out)
    return out


def kernel(
    heads,
    n_dp,
    rate_hbm,
    resets_hbm,
    pairs_hbm,
    q_hbm,
    k_hbm,
    v_hbm,
    g_hbm,
    do_hbm,
    gain_hbm,
    ret_hbm,
    dq_hbm,
    dk_hbm,
    dv_hbm,
    dgate_hbm,
    dgain_hbm,
    q_ref,
    k_ref,
    v_ref,
    g_ref,
    do_ref,
    ret_ref,
    dq_ref,
    dk_ref,
    dv_ref,
    dgate_ref,
    gain_ref,
    rate,
    resets,
    pairs,
    dgain_ref,
    l_buf,
    s_buf,
    e_buf,
    g_buf,
    eo_buf,
    no_buf,
    r1,
    o2,
    r3,
    o4,
    t_out,
    t_in,
    seed,
    b_out,
    c_out,
    c_in,
    b_in,
    f_in,
    start,
    dkp,
    dvp,
    gp,
    gz,
    gx_out,
    gx,
    gd_out,
    gd,
    ss,
    rs,
    xs,
    xr,
    hs,
    hr,
    cs,
    cr,
    bs,
    br,
    gs,
    gr,
    in_sem,
    out_sem,
):
    me = lax.axis_index("context")
    my_dp = lax.axis_index("dp")
    x, z = me // ROW, lax.rem(me, ROW)
    m = lax.rem(z, SPAN)
    side = z // SPAN
    is_prompt = jnp.logical_and(x >= 1, x <= 2)
    is_response = jnp.logical_not(is_prompt)
    second = x >= 2
    mirror = x + 1 - 2 * lax.rem(x, 2)
    first = jnp.logical_and(is_response, m == 0)
    scale = HD**-0.5

    def ctx(xx, zz):
        return xx * ROW + lax.rem(zz + 2 * ROW, ROW)

    def lent(h):
        return pick(LENT, h) == 1

    def owns(h):
        return lent(h) == is_response

    def both(a, b):
        return jnp.logical_and(a, b)

    loads = [
        pltpu.make_async_copy(src, dst, in_sem.at[i])
        for i, (src, dst) in enumerate(
            (
                (rate_hbm, rate),
                (resets_hbm, resets),
                (pairs_hbm, pairs),
                (k_hbm, k_ref),
                (v_hbm, v_ref),
                (q_hbm, q_ref),
                (g_hbm, g_ref),
                (do_hbm, do_ref),
                (gain_hbm, gain_ref),
            )
        )
    ]
    for load in loads:
        load.start()

    barrier = pltpu.get_barrier_semaphore()

    def greet(k, c):
        other = lax.rem(x + 2, ROWS) * ROW + z
        far = lax.rem(mirror + 2, ROWS) * ROW + z
        target = jnp.where(
            k < ROW,
            ctx(x, z + k),
            jnp.where(k < 2 * ROW, ctx(mirror, z + k), jnp.where(k == 2 * ROW, other, far)),
        )
        pl.semaphore_signal(barrier, inc=1, device_id={"context": target}, device_id_type=MESH)
        return c

    def greet_dp(k, c):
        pl.semaphore_signal(
            barrier, inc=1, device_id={"dp": lax.rem(my_dp + k, n_dp)}, device_id_type=MESH
        )
        return c

    lax.fori_loop(1, 2 * ROW + 2, greet, 0)
    lax.fori_loop(1, n_dp, greet_dp, 0)

    for load in loads[:3]:
        load.wait()

    prompt_index = jnp.clip(me - ROW, 0, 2 * ROW - 1)
    rho = jnp.where(is_prompt, resets[0, prompt_index], TOK)

    def cols(h):
        return pl.ds(pl.multiple_of(h * HD, HD), HD)

    def column_weights(h):
        lam = rate[h]
        t = lax.broadcasted_iota(jnp.int32, (TOK, 1), 0)
        tf = t.astype(F32)
        into = jnp.where(t < rho, jnp.exp(-lam * (tf + 1.0)), 0.0)
        out = jnp.where(t >= lax.rem(rho, TOK), jnp.exp(-lam * (TOK - 1.0 - tf)), 0.0)
        return into, out

    def decay_row(h):
        return jnp.exp(jnp.full((1, HD), -float(TOK) * rate[h], F32))

    def link(h, j, row):
        return row * (resets[0, j] == TOK).astype(F32)

    def rows_of(zz):
        return pl.ds(pl.multiple_of(zz * SL, SL), SL)

    def part(p):
        return pl.ds(pl.multiple_of(p * PR, PR), PR)

    def spread(piece, target_row, landing, phase, h):
        def one(k, c):
            src, zz = piece(k)
            remote(
                src,
                landing(k),
                ss.at[phase, h],
                rs.at[phase, h],
                context=target_row * ROW + zz,
            ).start()
            return c

        lax.fori_loop(1, ROW, one, 0)

        @pl.when(target_row != x)
        def _():
            one(0, 0)

    def to_owners(src, dst, phase, h):
        def piece(k):
            zz = lax.rem(z + k, ROW)
            return src.at[h, rows_of(zz)], zz

        spread(piece, jnp.where(lent(h), mirror, x), lambda k: dst.at[h, k], phase, h)

        @pl.when(jnp.logical_not(lent(h)))
        def _():
            dst[h, 0] = src[h, rows_of(z)]

    def from_owner(src, dst, phase, h):
        def piece(k):
            return src.at[h, k], lax.rem(z - k + ROW, ROW)

        spread(piece, jnp.where(lent(h), mirror, x), lambda k: dst.at[h, rows_of(z)], phase, h)

        @pl.when(jnp.logical_not(lent(h)))
        def _():
            dst[h, rows_of(z)] = src[h, 0]

    def wait_slices(phase, h, sent):
        for n, when in ((ROW, lent(h)), (ROW - 1, jnp.logical_not(lent(h)))):

            @pl.when(when)
            def _():
                ref = r1.at[h, pl.ds(0, n)]
                c = remote(ref, ref, ss.at[phase, h], rs.at[phase, h], context=me)
                if sent:
                    c.wait_send()
                else:
                    c.wait_recv()

    def wait_bytes(count, send_sem, recv_sem, sent):
        ref = r1.at[0, pl.ds(0, count)]
        c = remote(ref, ref, send_sem, recv_sem, context=me)
        if sent:
            c.wait_send()
        else:
            c.wait_recv()

    def stage_a(h, c):
        _, out = column_weights(h)
        kw = k_ref[:, cols(h)].astype(F32) * (out * scale)
        hi, lo = split(kw)
        vh = v_ref[:, cols(h)]
        l_buf[h] = dot(hi, vh, 0, 0) + dot(lo, vh, 0, 0)
        return c

    loads[3].wait()
    loads[4].wait()
    stage_a(0, 0)
    pl.semaphore_wait(barrier, 2 * ROW + 1 + n_dp - 1)

    def send_a(h, c):
        @pl.when(is_prompt)
        def _():
            to_owners(l_buf, r1, 0, h)

        @pl.when(h + 1 < heads)
        def _():
            stage_a(h + 1, 0)

        return c

    lax.fori_loop(0, heads, send_a, 0)

    def x_copy(src, dst, kind, h, xx):
        return remote(src, dst, xs.at[kind, h], xr.at[kind, h], context=xx * ROW + z)

    def hand_over(src, dst, kind, h, xx):
        @pl.when(xx != x)
        def _():
            x_copy(src, dst, kind, h, xx).start()

        @pl.when(xx == x)
        def _():
            dst[...] = src[...]

    def stage_b(h):
        wait_slices(0, h, False)

        @pl.when(second)
        def _():
            wait_bytes(1, xs.at[0, h], xr.at[0, h], False)
            start[...] = t_in[h]

        @pl.when(jnp.logical_not(second))
        def _():
            start[...] = jnp.zeros_like(start)

        row = decay_row(h)
        base = jnp.where(second, ROW, 0)

        def step(jz, carry):
            s, c0, c1 = carry
            j = base + jz
            slot = lax.rem(z - jz + ROW, ROW)
            o2[h, slot] = s
            s = s * link(h, j, row) + r1[h, slot]
            c0 = c0 + s * (pairs[0, 0] == j).astype(F32)
            c1 = c1 + s * (pairs[0, 1] == j).astype(F32)
            return s, c0, c1

        zero = jnp.zeros((SL, HD), F32)
        s, c0, c1 = lax.fori_loop(0, ROW, step, (start[...], zero, zero))
        c_out[h, 0] = c0
        c_out[h, 1] = c1

        @pl.when(jnp.logical_not(second))
        def _():
            t_out[h] = s
            x_copy(t_out.at[h], t_in.at[h], 0, h, jnp.where(lent(h), 3, 2)).start()

        half = second.astype(jnp.int32)
        hand_over(c_out.at[h, 0], c_in.at[h, half], 1, h, 0)
        hand_over(c_out.at[h, 1], c_in.at[h, half], 1, h, ROWS - 1)
        from_owner(o2, s_buf, 1, h)

    def wait_x(kind, h, sent):
        for n, when in ((1, lent(h)), (2, jnp.logical_not(lent(h)))):

            @pl.when(when)
            def _():
                wait_bytes(n, xs.at[kind, h], xr.at[kind, h], sent)

    def stage_seed(h):
        wait_x(1, h, False)
        seed[h] = c_in[h, 0] + c_in[h, 1]

        def one(sd, c):
            zz = sd * SPAN

            @pl.when(zz != z)
            def _():
                remote(
                    seed.at[h],
                    s_buf.at[h, rows_of(z)],
                    hs.at[0, h],
                    hr.at[0, h],
                    context=x * ROW + zz,
                ).start()

            @pl.when(zz == z)
            def _():
                s_buf[h, rows_of(z), :] = seed[h]

            return c

        lax.fori_loop(0, ROW // SPAN, one, 0)

    def chain(h):
        @pl.when(m == 0)
        def _():
            wait_bytes(ROW - 1, hs.at[0, h], hr.at[0, h], False)

        row = decay_row(h)

        def step(p, c):
            here = s_buf.at[h, part(p)]

            @pl.when(m > 0)
            def _():
                remote(here, here, cs.at[h, p], cr.at[h, p], context=me).wait_recv()

            @pl.when(m < SPAN - 1)
            def _():
                eo_buf[h, part(p), :] = s_buf[h, part(p), :] * row + l_buf[h, part(p), :]
                remote(
                    eo_buf.at[h, part(p)], here, cs.at[h, p], cr.at[h, p], context=me + 1
                ).start()

            return c

        lax.fori_loop(0, PARTS, step, 0)

    gp[...] = jnp.zeros_like(gp)
    for load in loads[5:]:
        load.wait()

    results = (
        (ret_ref, ret_hbm),
        (dq_ref, dq_hbm),
        (dk_ref, dk_hbm),
        (dv_ref, dv_hbm),
        (dgate_ref, dgate_hbm),
    )

    def store(h, *kinds):
        for i in kinds:
            src, dst = results[i]
            pltpu.make_async_copy(src.at[:, cols(h)], dst.at[:, cols(h)], out_sem.at[i]).start()

    def stage_c(h):
        lam = rate[h]
        into, out = column_weights(h)
        ti = lax.broadcasted_iota(jnp.int32, (TOK, TOK), 0)
        si = lax.broadcasted_iota(jnp.int32, (TOK, TOK), 1)
        dist = (ti - si).astype(F32)
        allowed = (ti >= si) & ((ti >= rho) == (si >= rho))
        mask = jnp.where(allowed, jnp.exp(-lam * jnp.maximum(dist, 0.0)), 0.0)
        qh, kh, vh = q_ref[:, cols(h)], k_ref[:, cols(h)], v_ref[:, cols(h)]
        weights = (dot(qh, kh, 1, 1) * scale * mask).astype(BF16)
        mixed = dot(weights, vh, 1, 0)
        s_hi, s_lo = split(s_buf[h])
        mixed = mixed + into * (dot(qh, s_hi, 1, 0) + dot(qh, s_lo, 1, 0))
        centre = mixed - jnp.mean(mixed, axis=1, keepdims=True)
        r = lax.rsqrt(jnp.mean(centre * centre, axis=1, keepdims=True) + 1e-05)
        xhat = centre * r
        gain = gain_ref[cols(h)].reshape(1, HD)
        gate = g_ref[:, cols(h)].astype(F32)
        go = do_ref[:, cols(h)].astype(F32)
        sig = 1.0 / (1.0 + jnp.exp(-gate))
        silu = gate * sig
        ret_ref[:, cols(h)] = (silu * xhat * gain).astype(BF16)
        gox = go * xhat
        dgate_ref[:, cols(h)] = (gox * gain * (sig + silu * (1.0 - sig))).astype(BF16)
        gp[pl.ds(h, 1), :] = jnp.sum(gox * silu, axis=0, keepdims=True)
        dx = go * silu * gain
        dx = dx - jnp.mean(dx, axis=1, keepdims=True) - xhat * jnp.mean(
            dx * xhat, axis=1, keepdims=True
        )
        gm = dx * r
        e_hi, e_lo = split(gm * into)
        e_buf[h] = dot(qh, e_hi, 0, 0) + dot(qh, e_lo, 0, 0)
        low, rest = split(gm)
        gw = (dot(low, vh, 1, 1) * mask).astype(BF16)
        inter = dot(low, s_hi, 1, 1) + dot(low, s_lo, 1, 1) + dot(rest, s_hi, 1, 1)
        dq_ref[:, cols(h)] = (dot(gw, kh, 1, 0) * scale + inter * into).astype(BF16)
        dkp[h] = dot(gw, qh, 0, 0) * scale
        dvp[h] = dot(weights, low, 0, 0)
        store(h, 0, 1, 4)

    def backward(h):
        @pl.when(m == SPAN - 1)
        def _():
            g_buf[h] = jnp.zeros((HD, HD), F32)

        row = decay_row(h)

        def step(p, c):
            here = g_buf.at[h, part(p)]

            @pl.when(m < SPAN - 1)
            def _():
                remote(here, here, bs.at[h, p], br.at[h, p], context=me).wait_recv()

            no_buf[h, part(p), :] = e_buf[h, part(p), :] + g_buf[h, part(p), :] * row

            @pl.when(m > 0)
            def _():
                remote(
                    no_buf.at[h, part(p)], here, bs.at[h, p], br.at[h, p], context=me - 1
                ).start()

            @pl.when(m == 0)
            def _():
                def one(k, cc):
                    zz = p * (ROW // PARTS) + k

                    @pl.when(zz != z)
                    def _():
                        remote(
                            no_buf.at[h, rows_of(zz)],
                            f_in.at[h, side],
                            hs.at[1, h],
                            hr.at[1, h],
                            context=x * ROW + zz,
                        ).start()

                    @pl.when(zz == z)
                    def _():
                        f_in[h, side] = no_buf[h, rows_of(zz), :]

                    return cc

                lax.fori_loop(0, ROW // PARTS, one, 0)

            return c

        lax.fori_loop(0, PARTS, step, 0)

    def stage_sum(h):
        @pl.when(m == 0)
        def _():
            wait_bytes(1, hs.at[1, h], hr.at[1, h], False)

        @pl.when(m > 0)
        def _():
            wait_bytes(2, hs.at[1, h], hr.at[1, h], False)

        b_out[h] = f_in[h, 0] + f_in[h, 1]
        pair = x // (ROWS - 1)
        for half in range(2):
            near = 2 - half
            target = jnp.where(lent(h), (1 - half) * (ROWS - 1), near)
            hand_over(b_out.at[h], b_in.at[h, pair], 3, h, target)

    def stage_d(h):
        wait_slices(2, h, False)
        wait_x(3, h, False)

        @pl.when(second)
        def _():
            start[...] = jnp.zeros_like(start)

        @pl.when(jnp.logical_not(second))
        def _():
            wait_bytes(1, xs.at[2, h], xr.at[2, h], False)
            start[...] = t_in[h]

        row = decay_row(h)
        base = jnp.where(second, ROW, 0)

        def step(i, g):
            jz = ROW - 1 - i
            j = base + jz
            slot = lax.rem(z - jz + ROW, ROW)
            g = g + b_in[h, 0] * (pairs[0, 0] == j).astype(F32)
            g = g + b_in[h, 1] * (pairs[0, 1] == j).astype(F32)
            o4[h, slot] = g
            return r3[h, slot] + g * link(h, j, row)

        g = lax.fori_loop(0, ROW, step, start[...])

        @pl.when(second)
        def _():
            t_out[h] = g
            x_copy(t_out.at[h], t_in.at[h], 2, h, jnp.where(lent(h), 0, 1)).start()

        from_owner(o4, g_buf, 3, h)

    def gain_row_send():
        def one(k, c):
            remote(gp, gz.at[z], gs.at[0], gr.at[0], context=ctx(x, z + k)).start()
            return c

        lax.fori_loop(1, ROW, one, 0)
        gz[z] = gp[...]

    def gain_x_send():
        ref = gz.at[pl.ds(0, ROW - 1)]
        remote(ref, ref, gs.at[0], gr.at[0], context=me).wait()
        gx_out[...] = lax.fori_loop(1, ROW, lambda i, a: a + gz[i], gz[0])

        def one(k, c):
            remote(
                gx_out, gx.at[x], gs.at[1], gr.at[1], context=lax.rem(x + k, ROWS) * ROW + z
            ).start()
            return c

        lax.fori_loop(1, ROWS, one, 0)
        gx[x] = gx_out[...]

    def gain_dp_send():
        ref = gx.at[pl.ds(0, ROWS - 1)]
        remote(ref, ref, gs.at[1], gr.at[1], context=me).wait()
        gd_out[...] = lax.fori_loop(1, ROWS, lambda i, a: a + gx[i], gx[0])

        def one(k, c):
            remote(
                gd_out, gd.at[my_dp], gs.at[2], gr.at[2], dp=lax.rem(my_dp + k, n_dp)
            ).start()
            return c

        lax.fori_loop(1, n_dp, one, 0)
        gd[my_dp] = gd_out[...]

    @pl.when(is_prompt)
    def _():
        def run_b(h, c):
            @pl.when(owns(h))
            def _():
                stage_b(h)

            return c

        lax.fori_loop(0, heads, run_b, 0)

    def valid(h):
        return both(h >= 0, h < heads)

    lag = jnp.where(is_prompt, 0, pick(LAG, m))
    lag_back = pick(LAG_BACK, m)

    def beat(i, c):
        @pl.when(is_response)
        def _():
            @pl.when(both(i < heads, owns(i)))
            def _():
                stage_b(i)

            @pl.when(valid(i - 1))
            def _():
                stage_seed(i - 1)

        hc = i - lag

        @pl.when(valid(hc))
        def _():
            @pl.when(is_prompt)
            def _():
                wait_slices(1, hc, False)

            @pl.when(is_response)
            def _():
                chain(hc)

            stage_c(hc)

            @pl.when(is_prompt)
            def _():
                to_owners(e_buf, r3, 2, hc)

        @pl.when(hc == heads)
        def _():
            gain_row_send()

        @pl.when(is_response)
        def _():
            hb = hc - lag_back

            @pl.when(valid(hb))
            def _():
                backward(hb)

            hg = i - LAG_SUM

            @pl.when(valid(hg))
            def _():
                stage_sum(hg)

        hd = i - jnp.where(is_response, LAG_LENT, LAG_OWNED)

        @pl.when(both(valid(hd), owns(hd)))
        def _():
            stage_d(hd)

        return c

    lax.fori_loop(0, heads + max(LAG_OWNED, LAG_LENT), beat, 0)
    gain_x_send()

    def stage_e(i, c):
        h = jnp.where(is_prompt, lax.rem(i + TURN, heads), i)
        @pl.when(is_prompt)
        def _():
            wait_slices(3, h, False)

        _, out = column_weights(h)
        out = out * scale
        g_hi, g_lo = split(g_buf[h])
        kh, vh = k_ref[:, cols(h)], v_ref[:, cols(h)]
        dk_ref[:, cols(h)] = (
            dkp[h] + out * (dot(vh, g_hi, 1, 1) + dot(vh, g_lo, 1, 1))
        ).astype(BF16)
        dv_ref[:, cols(h)] = (
            dvp[h] + out * (dot(kh, g_hi, 1, 0) + dot(kh, g_lo, 1, 0))
        ).astype(BF16)
        store(h, 2, 3)

        @pl.when(i == heads // 2)
        def _():
            gain_dp_send()

        return c

    lax.fori_loop(0, heads, stage_e, 0)

    w = gd.at[pl.ds(0, n_dp - 1)]
    remote(w, w, gs.at[2], gr.at[2], context=me).wait()
    token_total = TOK * ROW * ROWS * n_dp
    dgain_ref[...] = lax.fori_loop(1, n_dp, lambda i, a: a + gd[i], gd[0]) * (token_total**-0.5)
    last = pltpu.make_async_copy(dgain_ref, dgain_hbm, out_sem.at[5])
    last.start()

    def drain(h, c):
        @pl.when(is_prompt)
        def _():
            wait_slices(0, h, True)
            wait_slices(2, h, True)

        @pl.when(owns(h))
        def _():
            wait_slices(1, h, True)
            wait_slices(3, h, True)
            wait_x(1, h, True)

            @pl.when(second)
            def _():
                wait_bytes(1, xs.at[2, h], xr.at[2, h], True)

            @pl.when(jnp.logical_not(second))
            def _():
                wait_bytes(1, xs.at[0, h], xr.at[0, h], True)

        @pl.when(is_response)
        def _():
            wait_x(3, h, True)

            @pl.when(m == 0)
            def _():
                wait_bytes(1, hs.at[0, h], hr.at[0, h], True)
                wait_bytes(ROW - 1, hs.at[1, h], hr.at[1, h], True)

            @pl.when(m > 0)
            def _():
                wait_bytes(2, hs.at[0, h], hr.at[0, h], True)

            def step(p, cc):
                ref = no_buf.at[h, part(p)]

                @pl.when(m < SPAN - 1)
                def _():
                    remote(ref, ref, cs.at[h, p], cr.at[h, p], context=me).wait_send()

                @pl.when(m > 0)
                def _():
                    remote(ref, ref, bs.at[h, p], br.at[h, p], context=me).wait_send()

                return cc

            lax.fori_loop(0, PARTS, step, 0)

        return c

    lax.fori_loop(0, heads, drain, 0)
    for i, (src, dst) in enumerate(results):
        pltpu.make_async_copy(src, dst, out_sem.at[i]).wait()
    last.wait()


def finish_kernel(heads, *refs):
    given, out, held, total, sem_in, sem_out = (
        refs[:6],
        refs[6:12],
        refs[12:18],
        refs[18],
        refs[19],
        refs[20],
    )
    loads = [pltpu.make_async_copy(given[i], held[i], sem_in.at[i]) for i in range(6)]
    stores = [pltpu.make_async_copy(held[i], out[i], sem_out.at[i]) for i in range(5)]
    stores.append(pltpu.make_async_copy(total, out[5], sem_out.at[5]))
    for load in loads:
        load.start()
    for load, store in zip(loads[:5], stores):
        load.wait()
        store.start()
    loads[5].wait()
    for h in range(heads):
        total[pl.ds(h * HD, HD)] = held[5][pl.ds(h, 1), :].reshape(HD)
    stores[5].start()
    for store in stores:
        store.wait()


def solution(mesh):
    n_dp = mesh.shape["dp"]
    assert mesh.shape["context"] == ROW * ROWS

    def per_device(
        queries,
        key_rows,
        value_rows,
        gate_rows,
        out_grad,
        decay_rate,
        norm_gain,
        reset_offsets,
        pair_prompts,
    ):
        heads = decay_rate.shape[0]
        flat = jax.ShapeDtypeStruct(queries.shape, BF16)
        state = pltpu.VMEM((heads, HD, HD), F32)
        slots = pltpu.VMEM((heads, ROW, SL, HD), F32)
        piece = pltpu.VMEM((heads, SL, HD), F32)
        two = pltpu.VMEM((heads, 2, SL, HD), F32)
        part = pltpu.VMEM((heads, TOK, HD), F32)
        small = pltpu.VMEM((8, HD), F32)
        dma = pltpu.SemaphoreType.DMA
        hbm = pl.BlockSpec(memory_space=pltpu.HBM)
        anywhere = pl.BlockSpec(memory_space=pl.ANY)
        held = pltpu.VMEM(queries.shape, BF16)
        outs = pl.pallas_call(
            functools.partial(kernel, heads, n_dp),
            out_shape=(flat, flat, flat, flat, flat, jax.ShapeDtypeStruct((8, HD), F32)),
            in_specs=[hbm] * 9,
            out_specs=(hbm,) * 6,
            scratch_shapes=[held] * 10
            + [
                pltpu.VMEM(norm_gain.shape, F32),
                pltpu.SMEM(decay_rate.shape, F32),
                pltpu.SMEM(reset_offsets.shape, jnp.int32),
                pltpu.SMEM(pair_prompts.shape, jnp.int32),
                small,
            ]
            + [state] * 6
            + [slots] * 4
            + [piece] * 4
            + [two] * 4
            + [
                pltpu.VMEM((SL, HD), F32),
                part,
                part,
                small,
                pltpu.VMEM((ROW, 8, HD), F32),
                small,
                pltpu.VMEM((ROWS, 8, HD), F32),
                small,
                pltpu.VMEM((n_dp, 8, HD), F32),
                dma((4, heads)),
                dma((4, heads)),
                dma((4, heads)),
                dma((4, heads)),
                dma((2, heads)),
                dma((2, heads)),
                dma((heads, PARTS)),
                dma((heads, PARTS)),
                dma((heads, PARTS)),
                dma((heads, PARTS)),
                dma((3,)),
                dma((3,)),
                dma((9,)),
                dma((6,)),
            ],
            compiler_params=pltpu.CompilerParams(
                collective_id=0, has_side_effects=True, vmem_limit_bytes=60 << 20
            ),
        )(
            decay_rate,
            reset_offsets,
            pair_prompts,
            queries,
            key_rows,
            value_rows,
            gate_rows,
            out_grad,
            norm_gain,
        )
        total = jax.ShapeDtypeStruct(norm_gain.shape, F32)
        return pl.pallas_call(
            functools.partial(finish_kernel, heads),
            out_shape=(flat,) * 5 + (total,),
            in_specs=[anywhere] * 6,
            out_specs=(hbm,) * 6,
            scratch_shapes=[held] * 5
            + [small, pltpu.VMEM(norm_gain.shape, F32), dma((6,)), dma((6,))],
            compiler_params=pltpu.CompilerParams(vmem_limit_bytes=60 << 20),
        )(*outs)

    rows = P(("dp", "context"), "tensor")
    in_specs = (rows,) * 5 + (P("tensor"), P("tensor"), P("dp", None), P("dp", None))
    return jax.shard_map(
        per_device,
        mesh=mesh,
        in_specs=in_specs,
        out_specs=(rows,) * 5 + (P("tensor"),),
        check_vma=False,
    )
```
